32 devices in a mesh: dp: 8 (over z, x), head: 4 (over y, core).
Axes of the slice: x: 2, y: 2, z: 4, core: 2. Of those that a mesh axis runs over, the one named last changes fastest.
Arguments:
- queries: bfloat16 [4096, 2048], P('dp', 'head'), may hold values from -48 to 48
- encodings: bfloat16 [128, 128, 896], P('dp', None, 'head'), may hold values from -12 to 12
- neighbour_ids: int32 [64, 2], P('dp'), may hold values from 0 to 127, as said below
- block_place: int32 [128], replicated, may hold values from 0 to 127, as said below
- query_weight: bfloat16 [4096, 2048], P(None, 'head'), may hold values from -1 to 1
- key_weight: bfloat16 [896, 2048], P(None, 'head'), may hold values from -1 to 1
- value_weight: bfloat16 [896, 2048], P(None, 'head'), may hold values from -0.1875 to 0.1875
- attn_grad: bfloat16 [4096, 2048], P('dp', 'head'), may hold values from -24 to 24
Outputs:
- query_input_grad: bfloat16 [4096, 4096], P('dp', 'head')
- encodings_grad: bfloat16 [128, 128, 896], P('dp', None, 'head')
- key_weight_grad: float32 [896, 2048], P('dp', 'head')
- value_weight_grad: float32 [896, 2048], P('dp', 'head')
The draws below stay inside these ranges and needn't reach their ends.
Inputs may be any that keep to these rules, and one draw needn't show every extreme that they name: `neighbour_ids`: block b is stored at position block_place[b] of encodings, on the index block_place[b] // 16 of dp. Of the 16 slots of the spans of one index of dp, each index of dp stores the blocks of 2 or 1, and some index stores those of exactly 2. `block_place`: A permutation: every position once.
All inputs are finite; a program needn't handle non-finite values.
Results may differ from the reference program's by a relative error of at most 0.012.
The reference program's roundings to bfloat16 on the way count: a program that leaves them out, or rounds other values in their place, can miss the bound.
Values may be sent and summed in bfloat16 or wider, within the bound.
A program may use at most 128 MiB of HBM per device.

```python
import math
import jax
import jax.numpy as jnp
from jax import lax

D = 4096
HEADS = 16
DH = 128
E = 896
CH = 64
NTOK = 128
NEIGH = 2
CH_DEV = 8
HC = 2048
SPANS = 64
TOKENS = 4096
BLK_DEV = 16
BLOCKS = 128
N_DP = 8
N_HEAD = 4


def neighbour_plan(key):
    base = jax.random.fold_in(key, 501)
    key_order, key_first, key_second, key_names = jax.random.split(base, 4)
    slot_total = NEIGH * CH_DEV
    order = jax.vmap(lambda single: jax.random.permutation(single, N_DP))(jax.random.split(key_order, N_DP))
    owner_dev = order[:, jnp.arange(slot_total) % N_DP]
    first = jax.random.randint(key_first, (N_DP, slot_total), 0, BLK_DEV)
    second = jax.random.randint(key_second, (N_DP, slot_total), 0, BLK_DEV)
    position = (owner_dev * BLK_DEV + jnp.minimum(first, second)).astype(jnp.int32)
    id_at = jax.random.permutation(key_names, BLOCKS).astype(jnp.int32)
    place = jnp.argsort(id_at).astype(jnp.int32)
    block_names = id_at[position].reshape(SPANS, NEIGH).astype(jnp.int32)
    return (block_names, place)


def projections(key):
    key_query, key_key = jax.random.split(jax.random.fold_in(key, 502))
    query_proj = jnp.clip(jax.random.normal(key_query, (D, HEADS * DH), jnp.float32), -6.0, 6.0) / math.sqrt(D)
    key_proj = jnp.clip(jax.random.normal(key_key, (E, HEADS * DH), jnp.float32), -6.0, 6.0) / math.sqrt(E)
    return (query_proj, key_proj)


def draw_queries(key, part):
    values = jnp.clip(jax.random.normal(jax.random.fold_in(key, 504), (TOKENS, HEADS * DH), jnp.float32), -6.0, 6.0)
    return jnp.clip(values, -48.0, 48.0).astype(jnp.bfloat16)


def draw_encodings(key, part):
    values = jnp.clip(jax.random.normal(jax.random.fold_in(key, 506), (BLOCKS, NTOK, E), jnp.float32), -6.0, 6.0)
    return jnp.clip(values, -12.0, 12.0).astype(jnp.bfloat16)


def draw_neighbour_ids(key, part):
    return neighbour_plan(key)[0]


def draw_block_place(key, part):
    return neighbour_plan(key)[1]


def draw_query_weight(key, part):
    return projections(key)[0].astype(jnp.bfloat16)


def draw_key_weight(key, part):
    return projections(key)[1].astype(jnp.bfloat16)


def levels(rng, extent, cuts, smallest, high):
    def one(axis_at, shards_of):
        draws = jax.random.uniform(jax.random.fold_in(jax.random.fold_in(rng, 6), axis_at), (shards_of,), jnp.float32, smallest / len(cuts), high / len(cuts))
        return jnp.repeat(jnp.exp(draws), extent[axis_at] // shards_of).reshape((-1,) + (1,) * (len(extent) - axis_at - 1))

    level = one(*cuts[0])
    for cut in cuts[1:]:
        level = level * one(*cut)
    return level


def gaussian(key, extent, scale, most, shards=(), dtype=jnp.bfloat16):
    values = scale * jax.random.normal(key, extent, jnp.float32)
    if shards:
        values = values * levels(key, extent, shards, -0.22, 0.18)
    return jnp.clip(values, -most, most).astype(dtype)


def setup_inputs(seed: int = 0) -> dict:
    key_list = jax.random.split(jax.random.key(seed), 9)
    queries = draw_queries(jax.random.fold_in(key_list[8], 71), 0)
    encodings = draw_encodings(jax.random.fold_in(key_list[8], 71), 0)
    neighbour_ids = draw_neighbour_ids(jax.random.fold_in(key_list[8], 71), 0)
    block_place = draw_block_place(jax.random.fold_in(key_list[8], 71), 0)
    query_weight = draw_query_weight(jax.random.fold_in(key_list[8], 71), 0)
    key_weight = draw_key_weight(jax.random.fold_in(key_list[8], 71), 0)
    value_weight = gaussian(key_list[6], (E, HC), E ** -0.5, 0.1875, ((1, 4),))
    attn_grad = gaussian(key_list[7], (TOKENS, HC), 4.0, 24.0, ((0, 8), (1, 4)))
    return dict(queries=queries, encodings=encodings, neighbour_ids=neighbour_ids, block_place=block_place, query_weight=query_weight, key_weight=key_weight, value_weight=value_weight, attn_grad=attn_grad)


def span_grads(parts):
    query_rows = parts[0].astype(jnp.float32)
    key_rows = parts[1].astype(jnp.float32)
    value_rows = parts[2].astype(jnp.float32)
    grad_rows = parts[3].astype(jnp.float32)
    score_scale = 1.0 / math.sqrt(DH)
    scores = jnp.einsum('qhd,khd->hqk', query_rows, key_rows) * score_scale
    shifted = jnp.exp(scores - lax.optimization_barrier(jnp.max(scores, axis=-1, keepdims=True)))
    prob_rows = shifted / lax.optimization_barrier(jnp.sum(shifted, axis=-1, keepdims=True))
    prob_half = lax.optimization_barrier(prob_rows.astype(jnp.bfloat16)).astype(jnp.float32)
    grad_probs = jnp.einsum('qhd,khd->hqk', grad_rows, value_rows)
    row_delta = lax.optimization_barrier(jnp.sum(prob_rows * grad_probs, axis=-1, keepdims=True))
    grad_scores = (prob_rows * (grad_probs - row_delta) * score_scale).astype(jnp.bfloat16)
    grad_scores = lax.optimization_barrier(grad_scores).astype(jnp.float32)
    value_grad = jnp.einsum('hqk,qhd->khd', prob_half, grad_rows).astype(jnp.bfloat16)
    key_grad = jnp.einsum('hqk,qhd->khd', grad_scores, query_rows).astype(jnp.bfloat16)
    query_grad = jnp.einsum('hqk,khd->qhd', grad_scores, key_rows).astype(jnp.bfloat16)
    return (query_grad, key_grad, value_grad)

def reference(queries, encodings, neighbour_ids, block_place, query_weight, key_weight, value_weight, attn_grad):
    position = block_place[neighbour_ids.reshape(-1)].astype(jnp.int32)
    blocks = encodings[position]
    flat_rows = blocks.reshape(-1, E)
    keys = jnp.dot(flat_rows, key_weight, preferred_element_type=jnp.float32).astype(jnp.bfloat16)
    values = jnp.dot(flat_rows, value_weight, preferred_element_type=jnp.float32).astype(jnp.bfloat16)
    query_heads = queries.reshape(SPANS, CH, HEADS, DH)
    key_heads = keys.reshape(SPANS, NEIGH * NTOK, HEADS, DH)
    value_heads = values.reshape(SPANS, NEIGH * NTOK, HEADS, DH)
    grad_heads = attn_grad.reshape(SPANS, CH, HEADS, DH)
    query_grad, key_grad, value_grad = lax.map(span_grads, (query_heads, key_heads, value_heads, grad_heads))
    query_grad = query_grad.reshape(TOKENS, HC)
    key_flat = key_grad.reshape(-1, HC)
    value_flat = value_grad.reshape(-1, HC)
    group_cols = HC // N_HEAD
    input_total = jnp.zeros((TOKENS, D), jnp.float32)
    slot_total = jnp.zeros((flat_rows.shape[0], E), jnp.float32)
    for group in range(N_HEAD):
        low = group * group_cols
        high = low + group_cols
        query_part = jnp.dot(query_grad[:, low:high], query_weight[:, low:high].T, preferred_element_type=jnp.float32)
        input_total = input_total + query_part.astype(jnp.bfloat16).astype(jnp.float32)
        slot_part = jnp.dot(key_flat[:, low:high], key_weight[:, low:high].T, preferred_element_type=jnp.float32)
        slot_part = slot_part + jnp.dot(value_flat[:, low:high], value_weight[:, low:high].T, preferred_element_type=jnp.float32)
        slot_total = slot_total + slot_part.astype(jnp.bfloat16).astype(jnp.float32)
    query_input_grad = input_total.astype(jnp.bfloat16)
    key_weight_grad = jnp.dot(flat_rows.T, key_flat, preferred_element_type=jnp.float32)
    value_weight_grad = jnp.dot(flat_rows.T, value_flat, preferred_element_type=jnp.float32)
    slot_grad = slot_total.astype(jnp.bfloat16).reshape(NEIGH * SPANS, NTOK, E)
    summed = jnp.zeros((BLOCKS, NTOK, E), jnp.float32).at[position].add(slot_grad.astype(jnp.float32))
    return (query_input_grad, summed.astype(jnp.bfloat16), key_weight_grad, value_weight_grad)
```

```python
import functools
import math

import jax
import jax.numpy as jnp
from jax import lax
from jax.experimental import pallas as pl
from jax.experimental.pallas import tpu as pltpu
from jax.sharding import PartitionSpec as P

DH = 128
E = 896
CH = 64
NTOK = 128
NEIGH = 2


def plain_shards(
    queries,
    encodings,
    neighbour_ids,
    block_place,
    query_weight,
    key_weight,
    value_weight,
    attn_grad,
):
    dp_count = lax.axis_size("dp")
    own_blocks = encodings.shape[0]
    span_count = neighbour_ids.shape[0]
    block_names = neighbour_ids.reshape(-1)
    slot_count = block_names.shape[0]
    capacity = -(-slot_count // dp_count)
    position = block_place[block_names]
    owner_dev = position // own_blocks
    local_slot = position % own_blocks
    slot_order = jnp.arange(slot_count, dtype=jnp.int32)
    same_owner = (owner_dev[:, None] == owner_dev[None, :]) & (
        slot_order[None, :] < slot_order[:, None]
    )
    slot_rank = jnp.sum(same_owner.astype(jnp.int32), axis=1)
    device_match = owner_dev[:, None, None] == jnp.arange(dp_count, dtype=jnp.int32)[None, :, None]
    rank_match = slot_rank[:, None, None] == jnp.arange(capacity, dtype=jnp.int32)[None, None, :]
    requests = (
        jnp.sum(jnp.where(device_match & rank_match, local_slot[:, None, None] + 1, 0), axis=0) - 1
    )
    asked_rows = lax.all_to_all(requests, "dp", split_axis=0, concat_axis=0, tiled=True)
    valid_mask = asked_rows >= 0
    local_index = jnp.maximum(asked_rows, 0)
    blank = jnp.zeros((), jnp.bfloat16)
    packed = jnp.where(valid_mask[:, :, None, None], encodings[local_index], blank)
    received = lax.all_to_all(packed, "dp", split_axis=0, concat_axis=0, tiled=True)
    slot_blocks = lax.all_gather(received[owner_dev, slot_rank], "head", axis=2, tiled=True)
    flat_rows = slot_blocks.reshape(-1, E)
    both_weights = jnp.concatenate([key_weight, value_weight], axis=1)
    head_cols = key_weight.shape[1]
    local_heads = head_cols // DH
    projected = jnp.dot(flat_rows, both_weights, preferred_element_type=jnp.float32).astype(
        jnp.bfloat16
    )
    key_rows = projected[:, :head_cols].reshape(span_count, NEIGH * NTOK, local_heads, DH)
    value_rows = projected[:, head_cols:].reshape(span_count, NEIGH * NTOK, local_heads, DH)
    query_heads = queries.reshape(span_count, CH, local_heads, DH)
    grad_heads = attn_grad.reshape(span_count, CH, local_heads, DH)
    score_scale = 1.0 / math.sqrt(DH)
    scores = (
        jnp.einsum("cqhd,ckhd->chqk", query_heads, key_rows, preferred_element_type=jnp.float32)
        * score_scale
    )
    shifted = jnp.exp(scores - jnp.max(scores, axis=-1, keepdims=True))
    prob_rows = shifted / jnp.sum(shifted, axis=-1, keepdims=True)
    prob_half = prob_rows.astype(jnp.bfloat16)
    grad_probs = jnp.einsum(
        "cqhd,ckhd->chqk", grad_heads, value_rows, preferred_element_type=jnp.float32
    )
    row_delta = jnp.sum(prob_rows * grad_probs, axis=-1, keepdims=True)
    grad_scores = (prob_rows * (grad_probs - row_delta) * score_scale).astype(jnp.bfloat16)
    value_grad = jnp.einsum(
        "chqk,cqhd->ckhd", prob_half, grad_heads, preferred_element_type=jnp.float32
    ).astype(jnp.bfloat16)
    key_grad = jnp.einsum(
        "chqk,cqhd->ckhd", grad_scores, query_heads, preferred_element_type=jnp.float32
    ).astype(jnp.bfloat16)
    query_grad = jnp.einsum(
        "chqk,ckhd->cqhd", grad_scores, key_rows, preferred_element_type=jnp.float32
    ).astype(jnp.bfloat16)
    partial_input = jnp.dot(
        query_grad.reshape(-1, head_cols), query_weight.T, preferred_element_type=jnp.float32
    )
    query_input_grad = lax.psum_scatter(
        partial_input.astype(jnp.bfloat16), "head", scatter_dimension=1, tiled=True
    )
    both_grads = jnp.concatenate(
        [key_grad.reshape(-1, head_cols), value_grad.reshape(-1, head_cols)], axis=1
    )
    weight_grads = lax.psum_scatter(
        lax.dot_general(
            flat_rows, both_grads, (((0,), (0,)), ((), ())), preferred_element_type=jnp.float32
        ),
        "dp",
        scatter_dimension=0,
        tiled=True,
    )
    slot_partial = jnp.dot(both_grads, both_weights.T, preferred_element_type=jnp.float32).reshape(
        slot_count, NTOK, E
    )
    slot_grad = lax.psum_scatter(
        slot_partial.astype(jnp.bfloat16), "head", scatter_dimension=2, tiled=True
    )
    quarter = slot_grad.shape[2]
    outgoing = (
        jnp.zeros((dp_count, capacity, NTOK, quarter), jnp.bfloat16)
        .at[owner_dev, slot_rank]
        .set(slot_grad)
    )
    returned = lax.all_to_all(outgoing, "dp", split_axis=0, concat_axis=0, tiled=True)
    block_match = (
        local_index.reshape(-1)[None, :] == jnp.arange(own_blocks, dtype=jnp.int32)[:, None]
    )
    target = (block_match & valid_mask.reshape(-1)[None, :]).astype(jnp.bfloat16)
    encodings_grad = jnp.dot(
        target, returned.reshape(dp_count * capacity, -1), preferred_element_type=jnp.float32
    )
    encodings_grad = encodings_grad.reshape(own_blocks, NTOK, quarter).astype(jnp.bfloat16)
    return (
        query_input_grad,
        encodings_grad,
        weight_grads[:, :head_cols],
        weight_grads[:, head_cols:],
    )

MESH = pl.DeviceIdType.MESH
VMEM_LIMIT = 60 * 1024 * 1024


def remote(src, dst, send_sem, recv_sem, device):
    return pltpu.make_async_remote_copy(
        src_ref=src,
        dst_ref=dst,
        send_sem=send_sem,
        recv_sem=recv_sem,
        device_id=device,
        device_id_type=MESH,
    )


def greet(devices):
    barrier = pltpu.get_barrier_semaphore()
    for device in devices:
        pl.semaphore_signal(barrier, inc=1, device_id=device, device_id_type=MESH)
    pl.semaphore_wait(barrier, len(devices))


def places_kernel(n, mine_ref, all_ref, landed, send_sem, recv_sem):
    me = lax.axis_index("dp")
    greet([{"dp": lax.rem(me + k, n)} for k in range(1, n)])
    copies = []
    for k in range(1, n):
        copy = remote(
            mine_ref,
            landed.at[me],
            send_sem.at[k - 1],
            recv_sem.at[k - 1],
            {"dp": lax.rem(me + k, n)},
        )
        copy.start()
        copies.append(copy)
    for k in range(1, n):
        sender = lax.rem(me - k + n, n)
        remote(
            mine_ref, landed.at[sender], send_sem.at[k - 1], recv_sem.at[k - 1], {"dp": sender}
        ).wait_recv()
        all_ref[sender] = landed[sender]
    all_ref[me] = mine_ref[...]
    for copy in copies:
        copy.wait_send()


def gather_kernel(
    n, packed_ref, out_ref, local_sem, a_send, a_recv, y_send, y_recv, s_send, s_recv, f_send, f_recv
):
    me = lax.axis_index("dp")
    col = lax.axis_index("head")
    far = lax.rem(col + 2, 4)
    near = col + 1 - 2 * lax.rem(col, 2)
    far_near = lax.rem(near + 2, 4)
    own = pltpu.make_async_copy(packed_ref.at[me], out_ref.at[me, col], local_sem)
    own.start()
    greet([{"dp": lax.rem(me + k, n)} for k in range(1, n)] + [{"head": far}, {"head": near}])

    def first(k):
        return remote(
            packed_ref.at[lax.rem(me + k, n)],
            out_ref.at[me, col],
            a_send.at[k],
            a_recv.at[k],
            {"dp": lax.rem(me + k, n)},
        )

    def arrived(k):
        sender = lax.rem(me - k + n, n)
        return remote(
            packed_ref.at[sender], out_ref.at[sender, col], a_send.at[k], a_recv.at[k], {"dp": sender}
        )

    def across(k, feature, sems, target):
        sender = lax.rem(me - k + n, n)
        block = out_ref.at[sender, feature]
        return remote(block, block, sems[0].at[k], sems[1].at[k], {"head": target})

    y_sems, s_sems, f_sems = (y_send, y_recv), (s_send, s_recv), (f_send, f_recv)
    for k in range(1, n):
        first(k).start()
    own.wait()
    for k in range(n):
        if k:
            arrived(k).wait_recv()
        across(k, col, y_sems, far).start()
        across(k, col, s_sems, near).start()
    for k in range(n):
        across(k, far, y_sems, far).wait_recv()
        across(k, far, f_sems, near).start()
    for k in range(n):
        across(k, near, s_sems, near).wait_recv()
        across(k, far_near, f_sems, near).wait_recv()
    for k in range(n):
        if k:
            first(k).wait_send()
        across(k, col, y_sems, far).wait_send()
        across(k, col, s_sems, near).wait_send()
        across(k, far, f_sems, near).wait_send()


def dot(a, b, over_a, over_b):
    return lax.dot_general(
        a, b, (((over_a,), (over_b,)), ((), ())), preferred_element_type=jnp.float32
    )


def span_kernel(
    dev_ref, rank_ref, one_ref, two_ref, q_ref, g_ref, wk_ref, wv_ref, blocks_ref, grads_ref, dq_ref
):
    depth = wk_ref.shape[0]
    cols = wk_ref.shape[1]
    rows = jnp.concatenate(
        [one_ref[...].reshape(depth, NTOK), two_ref[...].reshape(depth, NTOK)], axis=1
    )
    blocks_ref[...] = rows
    keys = dot(rows, wk_ref[...], 0, 0).astype(jnp.bfloat16)
    values = dot(rows, wv_ref[...], 0, 0).astype(jnp.bfloat16)
    scale = 1.0 / math.sqrt(DH)
    for head in range(cols // DH):
        at = slice(head * DH, (head + 1) * DH)
        q, g, k, v = q_ref[:, at], g_ref[:, at], keys[:, at], values[:, at]
        scores = dot(q, k, 1, 1) * scale
        shifted = jnp.exp(scores - jnp.max(scores, axis=-1, keepdims=True))
        probs = shifted / jnp.sum(shifted, axis=-1, keepdims=True)
        dprobs = dot(g, v, 1, 1)
        delta = jnp.sum(probs * dprobs, axis=-1, keepdims=True)
        dscores = (probs * (dprobs - delta) * scale).astype(jnp.bfloat16)
        half = probs.astype(jnp.bfloat16)
        grads_ref[:, at] = dot(dscores, q, 0, 0).astype(jnp.bfloat16)
        grads_ref[:, cols + head * DH : cols + (head + 1) * DH] = dot(half, g, 0, 0).astype(
            jnp.bfloat16
        )
        dq_ref[:, at] = dot(dscores, k, 1, 0).astype(jnp.bfloat16)


def exchange_kernel(
    n,
    cap,
    slot_ref,
    blocks_hbm,
    grads_hbm,
    dq_hbm,
    qw_hbm,
    wk_hbm,
    wv_hbm,
    qi_ref,
    ret_ref,
    kw_ref,
    vw_ref,
    blocks,
    grads,
    dq,
    qw,
    wk,
    wv,
    load_sem,
    s_own,
    s_out,
    s_in,
    s_far,
    s_far_in,
    s_sum,
    s_back,
    s_back_in,
    q_own,
    q_out,
    q_in,
    q_far,
    q_far_in,
    w_own,
    w_out,
    w_in,
    w_far,
    w_far_in,
    ss_sem,
    sy_sem,
    a_sem,
    qs_sem,
    qy_sem,
    wx_sem,
    wz_sem,
):
    me = lax.axis_index("dp")
    col = lax.axis_index("head")
    high, low = col // 2, lax.rem(col, 2)
    far = {"head": lax.rem(col + 2, 4)}
    near = {"head": col + 1 - 2 * low}
    side, line = lax.rem(me, 2), me // 2
    lines = n // 2
    pair = {"dp": me + 1 - 2 * side}
    loads = [
        pltpu.make_async_copy(src, dst, load_sem.at[i])
        for i, (src, dst) in enumerate(
            [
                (wk_hbm, wk),
                (wv_hbm, wv),
                (grads_hbm, grads),
                (blocks_hbm, blocks),
                (dq_hbm, dq),
                (qw_hbm, qw),
            ]
        )
    ]
    for load in loads:
        load.start()
    greet([{"dp": lax.rem(me + k, n)} for k in range(1, n)] + [far, near])
    s_groups, quarter, s_cols = s_far.shape
    cols = wk.shape[1]
    q_groups, q_rows, q_cols = q_far.shape
    w_groups, w_rows, w_cols = w_own.shape[0], w_own.shape[2], w_own.shape[3]

    def f32(x):
        return x.astype(jnp.float32)

    def near_copy(out, landed, sems, i):
        return remote(out.at[i], landed.at[i], sems.at[0, i], sems.at[1, i], near)

    def far_copy(out, landed, sems, i):
        return remote(out.at[i], landed.at[i], sems.at[0, i], sems.at[1, i], far)

    def slot_terms(i):
        at = pl.ds(pl.multiple_of(i * s_cols, s_cols), s_cols)
        key_rows, value_rows = grads[at, :cols], grads[at, cols:]
        for part in range(2):
            for target, owner in ((s_out, 1 - low), (s_own, low)):
                rows = pl.ds(pl.multiple_of((2 * part + owner) * quarter, 16), quarter)
                term = dot(wk[rows, :], key_rows, 1, 1) + dot(wv[rows, :], value_rows, 1, 1)
                target[i, part] = term.astype(jnp.bfloat16)
        near_copy(s_out, s_in, ss_sem, i).start()

    def slot_pairs(i):
        near_copy(s_out, s_in, ss_sem, i).wait_recv()
        s_far[i] = (f32(s_own[i, 1 - high]) + f32(s_in[i, 1 - high])).astype(jnp.bfloat16)
        far_copy(s_far, s_far_in, sy_sem, i).start()

    def slot_sums(i):
        far_copy(s_far, s_far_in, sy_sem, i).wait_recv()
        total = (f32(s_own[i, high]) + f32(s_in[i, high]) + f32(s_far_in[i])).astype(jnp.bfloat16)
        per = s_cols // NTOK
        for j in range(per):
            s_sum[i * per + j] = total[:, j * NTOK : (j + 1) * NTOK]

    def query_terms(i):
        for part in range(2):
            for target, owner in ((q_out, 1 - low), (q_own, low)):
                start = (2 * part + owner) * (q_groups * q_cols) + i * q_cols
                rows = pl.ds(pl.multiple_of(start, q_cols), q_cols)
                target[i, part] = dot(dq[...], qw[rows, :], 1, 1).astype(jnp.bfloat16)
        near_copy(q_out, q_in, qs_sem, i).start()

    def query_pairs(i):
        near_copy(q_out, q_in, qs_sem, i).wait_recv()
        q_far[i] = (f32(q_own[i, 1 - high]) + f32(q_in[i, 1 - high])).astype(jnp.bfloat16)
        far_copy(q_far, q_far_in, qy_sem, i).start()

    def query_sums(i):
        far_copy(q_far, q_far_in, qy_sem, i).wait_recv()
        at = pl.ds(pl.multiple_of(i * q_cols, q_cols), q_cols)
        qi_ref[:, at] = (f32(q_own[i, high]) + f32(q_in[i, high]) + f32(q_far_in[i])).astype(
            jnp.bfloat16
        )

    def weight_dot(i, which):
        at = pl.ds(pl.multiple_of(i * w_cols, w_cols), w_cols)
        rows = blocks[:, which].reshape(lines * w_rows, blocks.shape[3])
        return dot(rows, grads[:, at], 1, 0).reshape(lines, w_rows, w_cols)

    def weight_copy(i):
        return remote(w_out.at[i], w_in.at[i], wx_sem.at[0, i], wx_sem.at[1, i], pair)

    def weight_send(i):
        w_out[i] = weight_dot(i, 1 - side).astype(jnp.bfloat16)
        weight_copy(i).start()

    def weight_keep(i):
        w_own[i] = weight_dot(i, side)

    def line_copy(i, k, sign):
        there = 2 * lax.rem(line + sign * k + lines, lines) + side
        return remote(
            w_far.at[i, k - 1],
            w_far_in.at[i, k - 1],
            wz_sem.at[0, i, k - 1],
            wz_sem.at[1, i, k - 1],
            {"dp": there},
        )

    def weight_pairs(i):
        weight_copy(i).wait_recv()
        for k in range(1, lines):
            there = lax.rem(line + k, lines)
            w_far[i, k - 1] = (w_own[i, there] + f32(w_in[i, there])).astype(jnp.bfloat16)
            line_copy(i, k, 1).start()

    def weight_sums(i):
        total = w_own[i, line] + f32(w_in[i, line])
        for k in range(1, lines):
            line_copy(i, k, -1).wait_recv()
            total = total + f32(w_far_in[i, k - 1])
        return total

    def back_copy(k):
        return remote(
            s_back.at[k - 1],
            s_back_in.at[k - 1],
            a_sem.at[0, k - 1],
            a_sem.at[1, k - 1],
            {"dp": lax.rem(me + k, n)},
        )

    def loop(start, count, body):
        def step(i, carry):
            body(i)
            return carry

        lax.fori_loop(start, count, step, 0)

    for load in loads[:3]:
        load.wait()
    slot_terms(0)

    def slot_step(i):
        slot_terms(i)
        slot_pairs(i - 1)

    loop(1, s_groups, slot_step)
    loads[3].wait()
    weight_send(0)
    slot_pairs(s_groups - 1)
    loop(1, w_groups, weight_send)
    loads[4].wait()
    loads[5].wait()
    query_terms(0)

    def query_step(i):
        query_terms(i)
        query_pairs(i - 1)

    loop(1, q_groups, query_step)
    loop(0, w_groups, weight_keep)
    query_pairs(q_groups - 1)
    loop(0, s_groups, slot_sums)
    for k in range(1, n):
        there = lax.rem(me + k, n)
        for r in range(cap):
            s_back[k - 1, r] = s_sum[slot_ref[there * cap + r]]
        back_copy(k).start()
    for r in range(cap):
        ret_ref[me, r] = s_sum[slot_ref[me * cap + r]]
    loop(0, w_groups, weight_pairs)
    loop(0, q_groups, query_sums)
    for i in range(w_groups):
        total = weight_sums(i)
        at = i * w_cols
        out, at = (kw_ref, at) if at < cols else (vw_ref, at - cols)
        out[:, at : at + w_cols] = total
    for k in range(1, n):
        back_copy(k).wait_recv()
        ret_ref[lax.rem(me - k + n, n)] = s_back_in[k - 1]

    def sent(i):
        near_copy(s_out, s_in, ss_sem, i).wait_send()
        far_copy(s_far, s_far_in, sy_sem, i).wait_send()

    loop(0, s_groups, sent)

    def query_sent(i):
        near_copy(q_out, q_in, qs_sem, i).wait_send()
        far_copy(q_far, q_far_in, qy_sem, i).wait_send()

    loop(0, q_groups, query_sent)

    def weight_sent(i):
        weight_copy(i).wait_send()
        for k in range(1, lines):
            line_copy(i, k, 1).wait_send()

    loop(0, w_groups, weight_sent)
    for k in range(1, n):
        back_copy(k).wait_send()


def scatter_kernel(index_ref, ret_ref, out_ref, total):
    total[...] = jnp.zeros_like(total)
    senders, cap = ret_ref.shape[:2]

    def add(i, carry):
        place = index_ref[i]

        @pl.when(place >= 0)
        def _():
            at = jnp.maximum(place, 0)
            total[at] += ret_ref[i // cap, i % cap].astype(jnp.float32)

        return carry

    lax.fori_loop(0, senders * cap, add, 0)

    def turn(i, carry):
        out_ref[i] = total[i].T.astype(jnp.bfloat16)
        return carry

    lax.fori_loop(0, total.shape[0], turn, 0)


def call(kernel, out_shape, scratch, collective=None, **kwargs):
    params = dict(vmem_limit_bytes=VMEM_LIMIT)
    if collective is not None:
        params.update(collective_id=collective, has_side_effects=True)
    return pl.pallas_call(
        kernel,
        out_shape=out_shape,
        scratch_shapes=scratch,
        compiler_params=pltpu.CompilerParams(**params),
        **kwargs,
    )


def shards(
    queries,
    encodings,
    neighbour_ids,
    block_place,
    query_weight,
    key_weight,
    value_weight,
    attn_grad,
):
    n = lax.axis_size("dp")
    bf16, f32, i32 = jnp.bfloat16, jnp.float32, jnp.int32
    own_blocks, _, quarter = encodings.shape
    spans = neighbour_ids.shape[0]
    slots = spans * NEIGH
    cap = -(-slots // n)
    me = lax.axis_index("dp")
    cols = key_weight.shape[1]
    depth = key_weight.shape[0]
    vmem = pl.BlockSpec(memory_space=pltpu.VMEM)
    anywhere = pl.BlockSpec(memory_space=pl.ANY)
    dma = pltpu.SemaphoreType.DMA
    sds = jax.ShapeDtypeStruct

    position = block_place[neighbour_ids.reshape(-1)]
    padded = jnp.zeros((8, 128), i32).at[0, :slots].set(position)
    places = call(
        functools.partial(places_kernel, n),
        sds((n, 8, 128), i32),
        [pltpu.VMEM((n, 8, 128), i32), dma((n - 1,)), dma((n - 1,))],
        collective=0,
        in_specs=[vmem],
        out_specs=vmem,
    )(padded)[:, 0, :slots]

    earlier = jnp.arange(slots, dtype=i32)[None, :] < jnp.arange(slots, dtype=i32)[:, None]
    ranks = jnp.arange(cap, dtype=i32)
    mine = (places // own_blocks) == me
    asked_rank = jnp.sum((mine[:, None, :] & earlier[None]).astype(i32), axis=2)
    pick = mine[:, None, :] & (asked_rank[:, None, :] == ranks[None, :, None])
    asked = jnp.sum(jnp.where(pick, (places % own_blocks)[:, None, :] + 1, 0), axis=2) - 1
    owner = position // own_blocks
    rank = jnp.sum(((owner[:, None] == owner[None, :]) & earlier).astype(i32), axis=1)
    chosen = (owner[None, None, :] == jnp.arange(n, dtype=i32)[:, None, None]) & (
        rank[None, None, :] == ranks[None, :, None]
    )
    slot_at = jnp.sum(jnp.where(chosen, jnp.arange(slots, dtype=i32), 0), axis=2).reshape(-1)

    packed = jnp.swapaxes(encodings, 1, 2)[jnp.maximum(asked, 0)]
    gathered = call(
        functools.partial(gather_kernel, n),
        sds((n, 4, cap, quarter, NTOK), bf16),
        [dma] + [dma((n,))] * 8,
        collective=1,
        in_specs=[anywhere],
        out_specs=anywhere,
    )(packed)

    def block_spec(j):
        return pl.BlockSpec(
            (1, 4, 1, quarter, NTOK),
            lambda i, dev, order: (dev[NEIGH * i + j], 0, order[NEIGH * i + j], 0, 0),
        )

    keys = NEIGH * NTOK
    tokens = spans * keys
    whole = pl.BlockSpec((depth, cols), lambda i, dev, order: (0, 0))
    per_span = pl.BlockSpec((CH, cols), lambda i, dev, order: (i, 0))
    blocks, grads, dq = call(
        span_kernel,
        [sds((depth, tokens), bf16), sds((tokens, 2 * cols), bf16), sds((spans * CH, cols), bf16)],
        (),
        grid_spec=pltpu.PrefetchScalarGridSpec(
            num_scalar_prefetch=2,
            grid=(spans,),
            in_specs=[block_spec(0), block_spec(1), per_span, per_span, whole, whole],
            out_specs=[
                pl.BlockSpec((depth, keys), lambda i, dev, order: (0, i)),
                pl.BlockSpec((keys, 2 * cols), lambda i, dev, order: (i, 0)),
                per_span,
            ],
        ),
    )(owner, rank, gathered, gathered, queries, attn_grad, key_weight, value_weight)

    lines, w_rows, groups = n // 2, depth // n, 4
    s_cols = tokens // groups
    q_rows = queries.shape[0]
    q_width = query_weight.shape[0] // 4
    q_cols = q_width // groups
    w_cols = 2 * cols // groups

    def buffer(*shape, dtype=bf16):
        return pltpu.VMEM(shape, dtype)

    scratch = [
        buffer(lines, 2, w_rows, tokens),
        buffer(tokens, 2 * cols),
        buffer(q_rows, cols),
        buffer(*query_weight.shape),
        buffer(depth, cols),
        buffer(depth, cols),
        dma((6,)),
        buffer(groups, 2, quarter, s_cols),
        buffer(groups, 2, quarter, s_cols),
        buffer(groups, 2, quarter, s_cols),
        buffer(groups, quarter, s_cols),
        buffer(groups, quarter, s_cols),
        buffer(slots, quarter, NTOK),
        buffer(n - 1, cap, quarter, NTOK),
        buffer(n - 1, cap, quarter, NTOK),
        buffer(groups, 2, q_rows, q_cols),
        buffer(groups, 2, q_rows, q_cols),
        buffer(groups, 2, q_rows, q_cols),
        buffer(groups, q_rows, q_cols),
        buffer(groups, q_rows, q_cols),
        buffer(groups, lines, w_rows, w_cols, dtype=f32),
        buffer(groups, lines, w_rows, w_cols),
        buffer(groups, lines, w_rows, w_cols),
        buffer(groups, lines - 1, w_rows, w_cols),
        buffer(groups, lines - 1, w_rows, w_cols),
        dma((2, groups)),
        dma((2, groups)),
        dma((2, n - 1)),
        dma((2, groups)),
        dma((2, groups)),
        dma((2, groups)),
        dma((2, groups, lines - 1)),
    ]
    query_input_grad, returned, key_grad, value_grad = call(
        functools.partial(exchange_kernel, n, cap),
        [
            sds((q_rows, q_width), bf16),
            sds((n, cap, quarter, NTOK), bf16),
            sds((w_rows, cols), f32),
            sds((w_rows, cols), f32),
        ],
        scratch,
        collective=2,
        in_specs=[pl.BlockSpec(memory_space=pltpu.SMEM)] + [anywhere] * 6,
        out_specs=[vmem] * 4,
    )(
        slot_at,
        blocks.reshape(lines, 2, w_rows, tokens),
        grads,
        dq,
        query_weight,
        key_weight,
        value_weight,
    )
    encodings_grad = call(
        scatter_kernel,
        sds(encodings.shape, bf16),
        [pltpu.VMEM((own_blocks, quarter, NTOK), f32)],
        in_specs=[pl.BlockSpec(memory_space=pltpu.SMEM), vmem],
        out_specs=vmem,
    )(asked.reshape(-1), returned)
    return query_input_grad, encodings_grad, key_grad, value_grad


def fits(mesh):
    dp, head = mesh.shape["dp"], mesh.shape["head"]
    return head == 4 and dp % 2 == 0 and dp > 2 and E % (16 * dp) == 0


def solution(mesh):
    in_specs = (
        P("dp", "head"),
        P("dp", None, "head"),
        P("dp", None),
        P(),
        P(None, "head"),
        P(None, "head"),
        P(None, "head"),
        P("dp", "head"),
    )
    out_specs = (P("dp", "head"), P("dp", None, "head"), P("dp", "head"), P("dp", "head"))
    return jax.shard_map(
        shards if fits(mesh) else plain_shards,
        mesh=mesh,
        in_specs=in_specs,
        out_specs=out_specs,
        check_vma=False,
    )
```

```python
import functools
import math

import jax
import jax.numpy as jnp
from jax import lax
from jax.experimental import pallas as pl
from jax.experimental.pallas import tpu as pltpu
from jax.sharding import PartitionSpec as P

DH = 128
E = 896
CH = 64
NTOK = 128
NEIGH = 2


def plain_shards(
    queries,
    encodings,
    neighbour_ids,
    block_place,
    query_weight,
    key_weight,
    value_weight,
    attn_grad,
):
    dp_count = lax.axis_size("dp")
    own_blocks = encodings.shape[0]
    span_count = neighbour_ids.shape[0]
    block_names = neighbour_ids.reshape(-1)
    slot_count = block_names.shape[0]
    capacity = -(-slot_count // dp_count)
    position = block_place[block_names]
    owner_dev = position // own_blocks
    local_slot = position % own_blocks
    slot_order = jnp.arange(slot_count, dtype=jnp.int32)
    same_owner = (owner_dev[:, None] == owner_dev[None, :]) & (
        slot_order[None, :] < slot_order[:, None]
    )
    slot_rank = jnp.sum(same_owner.astype(jnp.int32), axis=1)
    device_match = owner_dev[:, None, None] == jnp.arange(dp_count, dtype=jnp.int32)[None, :, None]
    rank_match = slot_rank[:, None, None] == jnp.arange(capacity, dtype=jnp.int32)[None, None, :]
    requests = (
        jnp.sum(jnp.where(device_match & rank_match, local_slot[:, None, None] + 1, 0), axis=0) - 1
    )
    asked_rows = lax.all_to_all(requests, "dp", split_axis=0, concat_axis=0, tiled=True)
    valid_mask = asked_rows >= 0
    local_index = jnp.maximum(asked_rows, 0)
    blank = jnp.zeros((), jnp.bfloat16)
    packed = jnp.where(valid_mask[:, :, None, None], encodings[local_index], blank)
    received = lax.all_to_all(packed, "dp", split_axis=0, concat_axis=0, tiled=True)
    slot_blocks = lax.all_gather(received[owner_dev, slot_rank], "head", axis=2, tiled=True)
    flat_rows = slot_blocks.reshape(-1, E)
    both_weights = jnp.concatenate([key_weight, value_weight], axis=1)
    head_cols = key_weight.shape[1]
    local_heads = head_cols // DH
    projected = jnp.dot(flat_rows, both_weights, preferred_element_type=jnp.float32).astype(
        jnp.bfloat16
    )
    key_rows = projected[:, :head_cols].reshape(span_count, NEIGH * NTOK, local_heads, DH)
    value_rows = projected[:, head_cols:].reshape(span_count, NEIGH * NTOK, local_heads, DH)
    query_heads = queries.reshape(span_count, CH, local_heads, DH)
    grad_heads = attn_grad.reshape(span_count, CH, local_heads, DH)
    score_scale = 1.0 / math.sqrt(DH)
    scores = (
        jnp.einsum("cqhd,ckhd->chqk", query_heads, key_rows, preferred_element_type=jnp.float32)
        * score_scale
    )
    shifted = jnp.exp(scores - jnp.max(scores, axis=-1, keepdims=True))
    prob_rows = shifted / jnp.sum(shifted, axis=-1, keepdims=True)
    prob_half = prob_rows.astype(jnp.bfloat16)
    grad_probs = jnp.einsum(
        "cqhd,ckhd->chqk", grad_heads, value_rows, preferred_element_type=jnp.float32
    )
    row_delta = jnp.sum(prob_rows * grad_probs, axis=-1, keepdims=True)
    grad_scores = (prob_rows * (grad_probs - row_delta) * score_scale).astype(jnp.bfloat16)
    value_grad = jnp.einsum(
        "chqk,cqhd->ckhd", prob_half, grad_heads, preferred_element_type=jnp.float32
    ).astype(jnp.bfloat16)
    key_grad = jnp.einsum(
        "chqk,cqhd->ckhd", grad_scores, query_heads, preferred_element_type=jnp.float32
    ).astype(jnp.bfloat16)
    query_grad = jnp.einsum(
        "chqk,ckhd->cqhd", grad_scores, key_rows, preferred_element_type=jnp.float32
    ).astype(jnp.bfloat16)
    partial_input = jnp.dot(
        query_grad.reshape(-1, head_cols), query_weight.T, preferred_element_type=jnp.float32
    )
    query_input_grad = lax.psum_scatter(
        partial_input.astype(jnp.bfloat16), "head", scatter_dimension=1, tiled=True
    )
    both_grads = jnp.concatenate(
        [key_grad.reshape(-1, head_cols), value_grad.reshape(-1, head_cols)], axis=1
    )
    weight_grads = lax.psum_scatter(
        lax.dot_general(
            flat_rows, both_grads, (((0,), (0,)), ((), ())), preferred_element_type=jnp.float32
        ),
        "dp",
        scatter_dimension=0,
        tiled=True,
    )
    slot_partial = jnp.dot(both_grads, both_weights.T, preferred_element_type=jnp.float32).reshape(
        slot_count, NTOK, E
    )
    slot_grad = lax.psum_scatter(
        slot_partial.astype(jnp.bfloat16), "head", scatter_dimension=2, tiled=True
    )
    quarter = slot_grad.shape[2]
    outgoing = (
        jnp.zeros((dp_count, capacity, NTOK, quarter), jnp.bfloat16)
        .at[owner_dev, slot_rank]
        .set(slot_grad)
    )
    returned = lax.all_to_all(outgoing, "dp", split_axis=0, concat_axis=0, tiled=True)
    block_match = (
        local_index.reshape(-1)[None, :] == jnp.arange(own_blocks, dtype=jnp.int32)[:, None]
    )
    target = (block_match & valid_mask.reshape(-1)[None, :]).astype(jnp.bfloat16)
    encodings_grad = jnp.dot(
        target, returned.reshape(dp_count * capacity, -1), preferred_element_type=jnp.float32
    )
    encodings_grad = encodings_grad.reshape(own_blocks, NTOK, quarter).astype(jnp.bfloat16)
    return (
        query_input_grad,
        encodings_grad,
        weight_grads[:, :head_cols],
        weight_grads[:, head_cols:],
    )

MESH = pl.DeviceIdType.MESH
VMEM_LIMIT = 60 * 1024 * 1024


def remote(src, dst, send_sem, recv_sem, device):
    return pltpu.make_async_remote_copy(
        src_ref=src,
        dst_ref=dst,
        send_sem=send_sem,
        recv_sem=recv_sem,
        device_id=device,
        device_id_type=MESH,
    )


def greet(devices):
    barrier = pltpu.get_barrier_semaphore()
    for device in devices:
        pl.semaphore_signal(barrier, inc=1, device_id=device, device_id_type=MESH)
    pl.semaphore_wait(barrier, len(devices))


def places_kernel(n, mine_ref, all_ref, landed, send_sem, recv_sem):
    me = lax.axis_index("dp")
    greet([{"dp": lax.rem(me + k, n)} for k in range(1, n)])
    copies = []
    for k in range(1, n):
        copy = remote(
            mine_ref,
            landed.at[me],
            send_sem.at[k - 1],
            recv_sem.at[k - 1],
            {"dp": lax.rem(me + k, n)},
        )
        copy.start()
        copies.append(copy)
    for k in range(1, n):
        sender = lax.rem(me - k + n, n)
        remote(
            mine_ref, landed.at[sender], send_sem.at[k - 1], recv_sem.at[k - 1], {"dp": sender}
        ).wait_recv()
        all_ref[sender] = landed[sender]
    all_ref[me] = mine_ref[...]
    for copy in copies:
        copy.wait_send()


def gather_steps(n, packed, got, local_sem, a_sem, y_sem, s_sem, f_sem, ready, project):
    me = lax.axis_index("dp")
    col = lax.axis_index("head")
    far = lax.rem(col + 2, 4)
    near = col + 1 - 2 * lax.rem(col, 2)
    far_near = lax.rem(near + 2, 4)
    ahead = 3

    def first(k):
        there = lax.rem(me + k, n)
        return remote(
            packed.at[there], got.at[me, col], a_sem.at[0, k], a_sem.at[1, k], {"dp": there}
        )

    def arrived(k):
        sender = lax.rem(me - k + n, n)
        return remote(
            packed.at[sender], got.at[sender, col], a_sem.at[0, k], a_sem.at[1, k], {"dp": sender}
        )

    def across(k, feature, sems, target):
        block = got.at[lax.rem(me - k + n, n), feature]
        return remote(block, block, sems.at[0, k], sems.at[1, k], {"head": target})

    own = pltpu.make_async_copy(packed.at[me], got.at[me, col], local_sem)
    own.start()
    for k in range(1, min(n, 1 + ahead)):
        first(k).start()
    own.wait()

    def spread(k):
        across(k, col, y_sem, far).start()
        across(k, col, s_sem, near).start()

    def pass_on(k):
        across(k, far, y_sem, far).wait_recv()
        across(k, far, f_sem, near).start()

    def take(k):
        across(k, near, s_sem, near).wait_recv()
        across(k, far_near, f_sem, near).wait_recv()
        project(lax.rem(me - k + n, n))

    spread(0)
    for k in range(1, n):
        arrived(k).wait_recv()
        spread(k)
        if k + ahead < n:
            first(k + ahead).start()
    pass_on(0)
    ready()

    def step(k, carry):
        pass_on(k)
        take(k - 1)
        return carry

    lax.fori_loop(1, n, step, 0)
    take(n - 1)

    def finish():
        for k in range(n):
            if k:
                first(k).wait_send()
            across(k, col, y_sem, far).wait_send()
            across(k, col, s_sem, near).wait_send()
            across(k, far, f_sem, near).wait_send()

    return finish


def dot(a, b, over_a, over_b):
    return lax.dot_general(
        a, b, (((over_a,), (over_b,)), ((), ())), preferred_element_type=jnp.float32
    )


def exchange_kernel(
    n,
    cap,
    dev_ref,
    rank_ref,
    slot_ref,
    packed_hbm,
    q_hbm,
    g_hbm,
    qw_hbm,
    wk_hbm,
    wv_hbm,
    qi_ref,
    ret_ref,
    kw_ref,
    vw_ref,
    got,
    kv,
    blocks,
    grads,
    dq,
    q,
    g,
    qw,
    wk,
    wv,
    load_sem,
    local_sem,
    ga_sem,
    gy_sem,
    gs_sem,
    gf_sem,
    s_own,
    s_out,
    s_in,
    s_far,
    s_far_in,
    s_sum,
    s_back,
    s_back_in,
    q_own,
    q_out,
    q_in,
    q_far,
    q_far_in,
    w_own,
    w_out,
    w_in,
    w_far,
    w_far_in,
    ss_sem,
    sy_sem,
    a_sem,
    qs_sem,
    qy_sem,
    wx_sem,
    wz_sem,
):
    me = lax.axis_index("dp")
    col = lax.axis_index("head")
    high, low = col // 2, lax.rem(col, 2)
    far = {"head": lax.rem(col + 2, 4)}
    near = {"head": col + 1 - 2 * low}
    side, line = lax.rem(me, 2), me // 2
    lines = n // 2
    pair = {"dp": me + 1 - 2 * side}
    loads = [
        pltpu.make_async_copy(src, dst, load_sem.at[i])
        for i, (src, dst) in enumerate(
            [
                (wk_hbm, wk),
                (wv_hbm, wv),
                (q_hbm, q),
                (g_hbm, g),
                (qw_hbm, qw),
            ]
        )
    ]
    for load in loads:
        load.start()
    greet([{"dp": lax.rem(me + k, n)} for k in range(1, n)] + [far, near])
    s_groups, quarter, s_cols = s_far.shape
    cols = wk.shape[1]
    q_groups, q_rows, q_cols = q_far.shape
    w_groups, w_rows, w_cols = w_own.shape[0], w_own.shape[2], w_own.shape[3]

    def f32(x):
        return x.astype(jnp.float32)

    def project(sender):
        rows = jnp.concatenate(
            [got[sender, :, r].reshape(wk.shape[0], NTOK) for r in range(cap)], axis=1
        )
        kv[sender, :, :, :cols] = (
            dot(rows, wk[...], 0, 0).astype(jnp.bfloat16).reshape(cap, NTOK, cols)
        )
        kv[sender, :, :, cols:] = (
            dot(rows, wv[...], 0, 0).astype(jnp.bfloat16).reshape(cap, NTOK, cols)
        )

    def weights_ready():
        for load in loads[:2]:
            load.wait()

    gather_sent = gather_steps(
        n, packed_hbm, got, local_sem, ga_sem, gy_sem, gs_sem, gf_sem, weights_ready, project
    )
    for load in loads[2:]:
        load.wait()

    def span(c):
        places = [(dev_ref[NEIGH * c + j], rank_ref[NEIGH * c + j]) for j in range(NEIGH)]
        keys = NEIGH * NTOK
        for j, (dev, rank) in enumerate(places):
            at = pl.ds(pl.multiple_of(c * keys + j * NTOK, NTOK), NTOK)
            blocks[:, :, :, at] = got[dev, :, rank].reshape(lines, 2, -1, NTOK)
        both = jnp.concatenate([kv[dev, rank] for dev, rank in places], axis=0)
        token_at = pl.ds(pl.multiple_of(c * CH, CH), CH)
        key_at = pl.ds(pl.multiple_of(c * keys, keys), keys)
        heads = [slice(h * DH, (h + 1) * DH) for h in range(cols // DH)]
        q_rows, g_rows = q[token_at, :], g[token_at, :]
        k_rows, v_rows = both[:, :cols], both[:, cols:]
        scale = 1.0 / math.sqrt(DH)
        scores = jnp.concatenate([dot(q_rows[:, at], k_rows[:, at], 1, 1) for at in heads], axis=0)
        dprobs = jnp.concatenate([dot(g_rows[:, at], v_rows[:, at], 1, 1) for at in heads], axis=0)
        scores = scores * scale
        shifted = jnp.exp(scores - jnp.max(scores, axis=-1, keepdims=True))
        probs = shifted * (1.0 / jnp.sum(shifted, axis=-1, keepdims=True))
        delta = jnp.sum(probs * dprobs, axis=-1, keepdims=True)
        dscores = (probs * (dprobs - delta) * scale).astype(jnp.bfloat16)
        half = probs.astype(jnp.bfloat16)
        for h, at in enumerate(heads):
            rows = slice(h * CH, (h + 1) * CH)
            grads[key_at, at] = dot(dscores[rows], q_rows[:, at], 0, 0).astype(jnp.bfloat16)
            grads[key_at, cols + at.start : cols + at.stop] = dot(
                half[rows], g_rows[:, at], 0, 0
            ).astype(jnp.bfloat16)
            dq[token_at, at] = dot(dscores[rows], k_rows[:, at], 1, 0).astype(jnp.bfloat16)

    def near_copy(out, landed, sems, i):
        return remote(out.at[i], landed.at[i], sems.at[0, i], sems.at[1, i], near)

    def far_copy(out, landed, sems, i):
        return remote(out.at[i], landed.at[i], sems.at[0, i], sems.at[1, i], far)

    def slot_terms(i):
        at = pl.ds(pl.multiple_of(i * s_cols, s_cols), s_cols)
        key_rows, value_rows = grads[at, :cols], grads[at, cols:]
        for part in range(2):
            for target, owner in ((s_out, 1 - low), (s_own, low)):
                rows = pl.ds(pl.multiple_of((2 * part + owner) * quarter, 16), quarter)
                term = dot(wk[rows, :], key_rows, 1, 1) + dot(wv[rows, :], value_rows, 1, 1)
                target[i, part] = term.astype(jnp.bfloat16)
        near_copy(s_out, s_in, ss_sem, i).start()

    def slot_pairs(i):
        near_copy(s_out, s_in, ss_sem, i).wait_recv()
        s_far[i] = (f32(s_own[i, 1 - high]) + f32(s_in[i, 1 - high])).astype(jnp.bfloat16)
        far_copy(s_far, s_far_in, sy_sem, i).start()

    def slot_sums(i):
        far_copy(s_far, s_far_in, sy_sem, i).wait_recv()
        total = (f32(s_own[i, high]) + f32(s_in[i, high]) + f32(s_far_in[i])).astype(jnp.bfloat16)
        per = s_cols // NTOK
        for j in range(per):
            s_sum[i * per + j] = total[:, j * NTOK : (j + 1) * NTOK]

    def query_terms(i):
        for part in range(2):
            for target, owner in ((q_out, 1 - low), (q_own, low)):
                start = (2 * part + owner) * (q_groups * q_cols) + i * q_cols
                rows = pl.ds(pl.multiple_of(start, q_cols), q_cols)
                target[i, part] = dot(dq[...], qw[rows, :], 1, 1).astype(jnp.bfloat16)
        near_copy(q_out, q_in, qs_sem, i).start()

    def query_pairs(i):
        near_copy(q_out, q_in, qs_sem, i).wait_recv()
        q_far[i] = (f32(q_own[i, 1 - high]) + f32(q_in[i, 1 - high])).astype(jnp.bfloat16)
        far_copy(q_far, q_far_in, qy_sem, i).start()

    def query_sums(i):
        far_copy(q_far, q_far_in, qy_sem, i).wait_recv()
        at = pl.ds(pl.multiple_of(i * q_cols, q_cols), q_cols)
        qi_ref[:, at] = (f32(q_own[i, high]) + f32(q_in[i, high]) + f32(q_far_in[i])).astype(
            jnp.bfloat16
        )

    def weight_dot(i, which):
        at = pl.ds(pl.multiple_of(i * w_cols, w_cols), w_cols)
        rows = blocks[:, which].reshape(lines * w_rows, blocks.shape[3])
        return dot(rows, grads[:, at], 1, 0).reshape(lines, w_rows, w_cols)

    def weight_copy(i):
        return remote(w_out.at[i], w_in.at[i], wx_sem.at[0, i], wx_sem.at[1, i], pair)

    def weight_send(i):
        w_out[i] = weight_dot(i, 1 - side).astype(jnp.bfloat16)
        weight_copy(i).start()

    def weight_keep(i):
        w_own[i] = weight_dot(i, side)

    def line_copy(i, k, sign):
        there = 2 * lax.rem(line + sign * k + lines, lines) + side
        return remote(
            w_far.at[i, k - 1],
            w_far_in.at[i, k - 1],
            wz_sem.at[0, i, k - 1],
            wz_sem.at[1, i, k - 1],
            {"dp": there},
        )

    def weight_pairs(i):
        weight_copy(i).wait_recv()
        for k in range(1, lines):
            there = lax.rem(line + k, lines)
            w_far[i, k - 1] = (w_own[i, there] + f32(w_in[i, there])).astype(jnp.bfloat16)
            line_copy(i, k, 1).start()

    def weight_sums(i):
        total = w_own[i, line] + f32(w_in[i, line])
        for k in range(1, lines):
            line_copy(i, k, -1).wait_recv()
            total = total + f32(w_far_in[i, k - 1])
        return total

    def back_copy(k):
        return remote(
            s_back.at[k - 1],
            s_back_in.at[k - 1],
            a_sem.at[0, k - 1],
            a_sem.at[1, k - 1],
            {"dp": lax.rem(me + k, n)},
        )

    def loop(start, count, body):
        def step(i, carry):
            body(i)
            return carry

        lax.fori_loop(start, count, step, 0)

    per_group = s_cols // (NEIGH * NTOK)

    def group(i):
        loop(i * per_group, (i + 1) * per_group, span)
        slot_terms(i)

    def group_step(i):
        group(i)
        slot_pairs(i - 1)

    group(0)
    loop(1, s_groups, group_step)
    loop(0, w_groups, weight_send)
    slot_pairs(s_groups - 1)
    query_terms(0)

    def query_step(i):
        query_terms(i)
        query_pairs(i - 1)

    loop(1, q_groups, query_step)
    loop(0, w_groups, weight_keep)
    query_pairs(q_groups - 1)
    loop(0, s_groups, slot_sums)
    for k in range(1, n):
        there = lax.rem(me + k, n)
        for r in range(cap):
            s_back[k - 1, r] = s_sum[slot_ref[there * cap + r]]
        back_copy(k).start()
    for r in range(cap):
        ret_ref[me, r] = s_sum[slot_ref[me * cap + r]]
    loop(0, w_groups, weight_pairs)
    loop(0, q_groups, query_sums)
    for i in range(w_groups):
        total = weight_sums(i)
        at = i * w_cols
        out, at = (kw_ref, at) if at < cols else (vw_ref, at - cols)
        out[:, at : at + w_cols] = total
    for k in range(1, n):
        back_copy(k).wait_recv()
        ret_ref[lax.rem(me - k + n, n)] = s_back_in[k - 1]

    def sent(i):
        near_copy(s_out, s_in, ss_sem, i).wait_send()
        far_copy(s_far, s_far_in, sy_sem, i).wait_send()

    loop(0, s_groups, sent)

    def query_sent(i):
        near_copy(q_out, q_in, qs_sem, i).wait_send()
        far_copy(q_far, q_far_in, qy_sem, i).wait_send()

    loop(0, q_groups, query_sent)

    def weight_sent(i):
        weight_copy(i).wait_send()
        for k in range(1, lines):
            line_copy(i, k, 1).wait_send()

    loop(0, w_groups, weight_sent)
    for k in range(1, n):
        back_copy(k).wait_send()
    gather_sent()


def scatter_kernel(index_ref, ret_ref, out_ref, total):
    total[...] = jnp.zeros_like(total)
    senders, cap = ret_ref.shape[:2]

    def add(i, carry):
        place = index_ref[i]

        @pl.when(place >= 0)
        def _():
            at = jnp.maximum(place, 0)
            total[at] += ret_ref[i // cap, i % cap].astype(jnp.float32)

        return carry

    lax.fori_loop(0, senders * cap, add, 0)

    def turn(i, carry):
        out_ref[i] = total[i].astype(jnp.bfloat16)
        return carry

    lax.fori_loop(0, total.shape[0], turn, 0)


def call(kernel, out_shape, scratch, collective=None, **kwargs):
    params = dict(vmem_limit_bytes=VMEM_LIMIT)
    if collective is not None:
        params.update(collective_id=collective, has_side_effects=True)
    return pl.pallas_call(
        kernel,
        out_shape=out_shape,
        scratch_shapes=scratch,
        compiler_params=pltpu.CompilerParams(**params),
        **kwargs,
    )


def shards(
    queries,
    encodings,
    neighbour_ids,
    block_place,
    query_weight,
    key_weight,
    value_weight,
    attn_grad,
):
    n = lax.axis_size("dp")
    bf16, f32, i32 = jnp.bfloat16, jnp.float32, jnp.int32
    own_blocks, _, quarter = encodings.shape
    spans = neighbour_ids.shape[0]
    slots = spans * NEIGH
    cap = -(-slots // n)
    me = lax.axis_index("dp")
    cols = key_weight.shape[1]
    depth = key_weight.shape[0]
    vmem = pl.BlockSpec(memory_space=pltpu.VMEM)
    anywhere = pl.BlockSpec(memory_space=pl.ANY)
    dma = pltpu.SemaphoreType.DMA
    sds = jax.ShapeDtypeStruct

    position = block_place[neighbour_ids.reshape(-1)]
    padded = jnp.zeros((8, 128), i32).at[0, :slots].set(position)
    places = call(
        functools.partial(places_kernel, n),
        sds((n, 8, 128), i32),
        [pltpu.VMEM((n, 8, 128), i32), dma((n - 1,)), dma((n - 1,))],
        collective=0,
        in_specs=[vmem],
        out_specs=vmem,
    )(padded)[:, 0, :slots]

    earlier = jnp.arange(slots, dtype=i32)[None, :] < jnp.arange(slots, dtype=i32)[:, None]
    ranks = jnp.arange(cap, dtype=i32)
    mine = (places // own_blocks) == me
    asked_rank = jnp.sum((mine[:, None, :] & earlier[None]).astype(i32), axis=2)
    pick = mine[:, None, :] & (asked_rank[:, None, :] == ranks[None, :, None])
    asked = jnp.sum(jnp.where(pick, (places % own_blocks)[:, None, :] + 1, 0), axis=2) - 1
    owner = position // own_blocks
    rank = jnp.sum(((owner[:, None] == owner[None, :]) & earlier).astype(i32), axis=1)
    chosen = (owner[None, None, :] == jnp.arange(n, dtype=i32)[:, None, None]) & (
        rank[None, None, :] == ranks[None, :, None]
    )
    slot_at = jnp.sum(jnp.where(chosen, jnp.arange(slots, dtype=i32), 0), axis=2).reshape(-1)

    packed = jnp.swapaxes(encodings, 1, 2)[jnp.maximum(asked, 0)]
    tokens = slots * NTOK
    lines, w_rows, groups = n // 2, depth // n, 4
    s_cols = tokens // groups
    q_rows = queries.shape[0]
    q_width = query_weight.shape[0] // 4
    q_cols = q_width // groups
    w_cols = 2 * cols // groups

    def buffer(*shape, dtype=bf16):
        return pltpu.VMEM(shape, dtype)

    scratch = [
        buffer(n, 4, cap, quarter, NTOK),
        buffer(n, cap, NTOK, 2 * cols),
        buffer(lines, 2, w_rows, tokens),
        buffer(tokens, 2 * cols),
        buffer(q_rows, cols),
        buffer(q_rows, cols),
        buffer(q_rows, cols),
        buffer(*query_weight.shape),
        buffer(depth, cols),
        buffer(depth, cols),
        dma((5,)),
        dma,
        dma((2, n)),
        dma((2, n)),
        dma((2, n)),
        dma((2, n)),
        buffer(groups, 2, quarter, s_cols),
        buffer(groups, 2, quarter, s_cols),
        buffer(groups, 2, quarter, s_cols),
        buffer(groups, quarter, s_cols),
        buffer(groups, quarter, s_cols),
        buffer(slots, quarter, NTOK),
        buffer(n - 1, cap, quarter, NTOK),
        buffer(n - 1, cap, quarter, NTOK),
        buffer(groups, 2, q_rows, q_cols),
        buffer(groups, 2, q_rows, q_cols),
        buffer(groups, 2, q_rows, q_cols),
        buffer(groups, q_rows, q_cols),
        buffer(groups, q_rows, q_cols),
        buffer(groups, lines, w_rows, w_cols, dtype=f32),
        buffer(groups, lines, w_rows, w_cols),
        buffer(groups, lines, w_rows, w_cols),
        buffer(groups, lines - 1, w_rows, w_cols),
        buffer(groups, lines - 1, w_rows, w_cols),
        dma((2, groups)),
        dma((2, groups)),
        dma((2, n - 1)),
        dma((2, groups)),
        dma((2, groups)),
        dma((2, groups)),
        dma((2, groups, lines - 1)),
    ]
    query_input_grad, returned, key_grad, value_grad = call(
        functools.partial(exchange_kernel, n, cap),
        [
            sds((q_rows, q_width), bf16),
            sds((n, cap, quarter, NTOK), bf16),
            sds((w_rows, cols), f32),
            sds((w_rows, cols), f32),
        ],
        scratch,
        collective=1,
        in_specs=[pl.BlockSpec(memory_space=pltpu.SMEM)] * 3 + [anywhere] * 6,
        out_specs=[vmem] * 4,
    )(
        owner,
        rank,
        slot_at,
        packed,
        queries,
        attn_grad,
        query_weight,
        key_weight,
        value_weight,
    )
    encodings_grad = call(
        scatter_kernel,
        sds((own_blocks, quarter, NTOK), bf16),
        [pltpu.VMEM((own_blocks, quarter, NTOK), f32)],
        in_specs=[pl.BlockSpec(memory_space=pltpu.SMEM), vmem],
        out_specs=vmem,
    )(asked.reshape(-1), returned)
    return query_input_grad, jnp.swapaxes(encodings_grad, 1, 2), key_grad, value_grad


def fits(mesh):
    dp, head = mesh.shape["dp"], mesh.shape["head"]
    return head == 4 and dp % 2 == 0 and dp > 2 and E % (16 * dp) == 0


def solution(mesh):
    in_specs = (
        P("dp", "head"),
        P("dp", None, "head"),
        P("dp", None),
        P(),
        P(None, "head"),
        P(None, "head"),
        P(None, "head"),
        P("dp", "head"),
    )
    out_specs = (P("dp", "head"), P("dp", None, "head"), P("dp", "head"), P("dp", "head"))
    return jax.shard_map(
        shards if fits(mesh) else plain_shards,
        mesh=mesh,
        in_specs=in_specs,
        out_specs=out_specs,
        check_vma=False,
    )
```

```python
import functools
import math

import jax
import jax.numpy as jnp
from jax import lax
from jax.experimental import pallas as pl
from jax.experimental.pallas import tpu as pltpu
from jax.sharding import PartitionSpec as P

DH = 128
E = 896
CH = 64
NTOK = 128
NEIGH = 2


def plain_shards(
    queries,
    encodings,
    neighbour_ids,
    block_place,
    query_weight,
    key_weight,
    value_weight,
    attn_grad,
):
    dp_count = lax.axis_size("dp")
    own_blocks = encodings.shape[0]
    span_count = neighbour_ids.shape[0]
    block_names = neighbour_ids.reshape(-1)
    slot_count = block_names.shape[0]
    capacity = -(-slot_count // dp_count)
    position = block_place[block_names]
    owner_dev = position // own_blocks
    local_slot = position % own_blocks
    slot_order = jnp.arange(slot_count, dtype=jnp.int32)
    same_owner = (owner_dev[:, None] == owner_dev[None, :]) & (
        slot_order[None, :] < slot_order[:, None]
    )
    slot_rank = jnp.sum(same_owner.astype(jnp.int32), axis=1)
    device_match = owner_dev[:, None, None] == jnp.arange(dp_count, dtype=jnp.int32)[None, :, None]
    rank_match = slot_rank[:, None, None] == jnp.arange(capacity, dtype=jnp.int32)[None, None, :]
    requests = (
        jnp.sum(jnp.where(device_match & rank_match, local_slot[:, None, None] + 1, 0), axis=0) - 1
    )
    asked_rows = lax.all_to_all(requests, "dp", split_axis=0, concat_axis=0, tiled=True)
    valid_mask = asked_rows >= 0
    local_index = jnp.maximum(asked_rows, 0)
    blank = jnp.zeros((), jnp.bfloat16)
    packed = jnp.where(valid_mask[:, :, None, None], encodings[local_index], blank)
    received = lax.all_to_all(packed, "dp", split_axis=0, concat_axis=0, tiled=True)
    slot_blocks = lax.all_gather(received[owner_dev, slot_rank], "head", axis=2, tiled=True)
    flat_rows = slot_blocks.reshape(-1, E)
    both_weights = jnp.concatenate([key_weight, value_weight], axis=1)
    head_cols = key_weight.shape[1]
    local_heads = head_cols // DH
    projected = jnp.dot(flat_rows, both_weights, preferred_element_type=jnp.float32).astype(
        jnp.bfloat16
    )
    key_rows = projected[:, :head_cols].reshape(span_count, NEIGH * NTOK, local_heads, DH)
    value_rows = projected[:, head_cols:].reshape(span_count, NEIGH * NTOK, local_heads, DH)
    query_heads = queries.reshape(span_count, CH, local_heads, DH)
    grad_heads = attn_grad.reshape(span_count, CH, local_heads, DH)
    score_scale = 1.0 / math.sqrt(DH)
    scores = (
        jnp.einsum("cqhd,ckhd->chqk", query_heads, key_rows, preferred_element_type=jnp.float32)
        * score_scale
    )
    shifted = jnp.exp(scores - jnp.max(scores, axis=-1, keepdims=True))
    prob_rows = shifted / jnp.sum(shifted, axis=-1, keepdims=True)
    prob_half = prob_rows.astype(jnp.bfloat16)
    grad_probs = jnp.einsum(
        "cqhd,ckhd->chqk", grad_heads, value_rows, preferred_element_type=jnp.float32
    )
    row_delta = jnp.sum(prob_rows * grad_probs, axis=-1, keepdims=True)
    grad_scores = (prob_rows * (grad_probs - row_delta) * score_scale).astype(jnp.bfloat16)
    value_grad = jnp.einsum(
        "chqk,cqhd->ckhd", prob_half, grad_heads, preferred_element_type=jnp.float32
    ).astype(jnp.bfloat16)
    key_grad = jnp.einsum(
        "chqk,cqhd->ckhd", grad_scores, query_heads, preferred_element_type=jnp.float32
    ).astype(jnp.bfloat16)
    query_grad = jnp.einsum(
        "chqk,ckhd->cqhd", grad_scores, key_rows, preferred_element_type=jnp.float32
    ).astype(jnp.bfloat16)
    partial_input = jnp.dot(
        query_grad.reshape(-1, head_cols), query_weight.T, preferred_element_type=jnp.float32
    )
    query_input_grad = lax.psum_scatter(
        partial_input.astype(jnp.bfloat16), "head", scatter_dimension=1, tiled=True
    )
    both_grads = jnp.concatenate(
        [key_grad.reshape(-1, head_cols), value_grad.reshape(-1, head_cols)], axis=1
    )
    weight_grads = lax.psum_scatter(
        lax.dot_general(
            flat_rows, both_grads, (((0,), (0,)), ((), ())), preferred_element_type=jnp.float32
        ),
        "dp",
        scatter_dimension=0,
        tiled=True,
    )
    slot_partial = jnp.dot(both_grads, both_weights.T, preferred_element_type=jnp.float32).reshape(
        slot_count, NTOK, E
    )
    slot_grad = lax.psum_scatter(
        slot_partial.astype(jnp.bfloat16), "head", scatter_dimension=2, tiled=True
    )
    quarter = slot_grad.shape[2]
    outgoing = (
        jnp.zeros((dp_count, capacity, NTOK, quarter), jnp.bfloat16)
        .at[owner_dev, slot_rank]
        .set(slot_grad)
    )
    returned = lax.all_to_all(outgoing, "dp", split_axis=0, concat_axis=0, tiled=True)
    block_match = (
        local_index.reshape(-1)[None, :] == jnp.arange(own_blocks, dtype=jnp.int32)[:, None]
    )
    target = (block_match & valid_mask.reshape(-1)[None, :]).astype(jnp.bfloat16)
    encodings_grad = jnp.dot(
        target, returned.reshape(dp_count * capacity, -1), preferred_element_type=jnp.float32
    )
    encodings_grad = encodings_grad.reshape(own_blocks, NTOK, quarter).astype(jnp.bfloat16)
    return (
        query_input_grad,
        encodings_grad,
        weight_grads[:, :head_cols],
        weight_grads[:, head_cols:],
    )

MESH = pl.DeviceIdType.MESH
VMEM_LIMIT = 60 * 1024 * 1024


def remote(src, dst, send_sem, recv_sem, device):
    return pltpu.make_async_remote_copy(
        src_ref=src,
        dst_ref=dst,
        send_sem=send_sem,
        recv_sem=recv_sem,
        device_id=device,
        device_id_type=MESH,
    )


def greet(devices):
    barrier = pltpu.get_barrier_semaphore()
    for device in devices:
        pl.semaphore_signal(barrier, inc=1, device_id=device, device_id_type=MESH)
    pl.semaphore_wait(barrier, len(devices))


def places_kernel(n, mine_ref, all_ref, landed, send_sem, recv_sem):
    me = lax.axis_index("dp")
    greet([{"dp": lax.rem(me + k, n)} for k in range(1, n)])
    copies = []
    for k in range(1, n):
        copy = remote(
            mine_ref,
            landed.at[me],
            send_sem.at[k - 1],
            recv_sem.at[k - 1],
            {"dp": lax.rem(me + k, n)},
        )
        copy.start()
        copies.append(copy)
    for k in range(1, n):
        sender = lax.rem(me - k + n, n)
        remote(
            mine_ref, landed.at[sender], send_sem.at[k - 1], recv_sem.at[k - 1], {"dp": sender}
        ).wait_recv()
        all_ref[sender] = landed[sender]
    all_ref[me] = mine_ref[...]
    for copy in copies:
        copy.wait_send()


def gather_steps(n, packed, got, local_sem, a_sem, y_sem, s_sem, f_sem, ready, project):
    me = lax.axis_index("dp")
    col = lax.axis_index("head")
    far = lax.rem(col + 2, 4)
    near = col + 1 - 2 * lax.rem(col, 2)
    far_near = lax.rem(near + 2, 4)
    ahead = 3

    def first(k):
        there = lax.rem(me + k, n)
        return remote(
            packed.at[there], got.at[me, col], a_sem.at[0, k], a_sem.at[1, k], {"dp": there}
        )

    def arrived(k):
        sender = lax.rem(me - k + n, n)
        return remote(
            packed.at[sender], got.at[sender, col], a_sem.at[0, k], a_sem.at[1, k], {"dp": sender}
        )

    def across(k, feature, sems, target):
        block = got.at[lax.rem(me - k + n, n), feature]
        return remote(block, block, sems.at[0, k], sems.at[1, k], {"head": target})

    own = pltpu.make_async_copy(packed.at[me], got.at[me, col], local_sem)
    own.start()
    for k in range(1, min(n, 1 + ahead)):
        first(k).start()
    own.wait()

    def spread(k):
        across(k, col, y_sem, far).start()
        across(k, col, s_sem, near).start()

    def pass_on(k):
        across(k, far, y_sem, far).wait_recv()
        across(k, far, f_sem, near).start()

    def take(k):
        across(k, near, s_sem, near).wait_recv()
        across(k, far_near, f_sem, near).wait_recv()
        project(lax.rem(me - k + n, n))

    spread(0)
    for k in range(1, n):
        arrived(k).wait_recv()
        spread(k)
        if k + ahead < n:
            first(k + ahead).start()
    pass_on(0)
    ready()

    def step(k, carry):
        pass_on(k)
        take(k - 1)
        return carry

    lax.fori_loop(1, n, step, 0)
    take(n - 1)

    def finish():
        for k in range(n):
            if k:
                first(k).wait_send()
            across(k, col, y_sem, far).wait_send()
            across(k, col, s_sem, near).wait_send()
            across(k, far, f_sem, near).wait_send()

    return finish


def dot(a, b, over_a, over_b):
    return lax.dot_general(
        a, b, (((over_a,), (over_b,)), ((), ())), preferred_element_type=jnp.float32
    )


def exchange_kernel(
    n,
    cap,
    dev_ref,
    rank_ref,
    slot_ref,
    packed_hbm,
    q_hbm,
    g_hbm,
    qw_hbm,
    wk_hbm,
    wv_hbm,
    qi_ref,
    ret_ref,
    kw_ref,
    vw_ref,
    got,
    kv,
    blocks,
    grads,
    dq,
    q,
    g,
    qw,
    wk,
    wv,
    load_sem,
    local_sem,
    ga_sem,
    gy_sem,
    gs_sem,
    gf_sem,
    s_own,
    s_out,
    s_in,
    s_far,
    s_far_in,
    s_sum,
    s_back,
    s_back_in,
    q_own,
    q_out,
    q_in,
    q_far,
    q_far_in,
    w_own,
    w_out,
    w_in,
    w_far,
    w_far_in,
    ss_sem,
    sy_sem,
    a_sem,
    qs_sem,
    qy_sem,
    wx_sem,
    wz_sem,
):
    me = lax.axis_index("dp")
    col = lax.axis_index("head")
    high, low = col // 2, lax.rem(col, 2)
    far = {"head": lax.rem(col + 2, 4)}
    near = {"head": col + 1 - 2 * low}
    side, line = lax.rem(me, 2), me // 2
    lines = n // 2
    pair = {"dp": me + 1 - 2 * side}
    loads = [
        pltpu.make_async_copy(src, dst, load_sem.at[i])
        for i, (src, dst) in enumerate(
            [
                (wk_hbm, wk),
                (wv_hbm, wv),
                (q_hbm, q),
                (g_hbm, g),
                (qw_hbm, qw),
            ]
        )
    ]
    for load in loads:
        load.start()
    greet([{"dp": lax.rem(me + k, n)} for k in range(1, n)] + [far, near])
    s_groups, quarter, s_cols = s_far.shape
    cols = wk.shape[1]
    q_groups, q_rows, q_cols = q_far.shape
    w_groups, w_rows, w_cols = w_own.shape[0], w_own.shape[2], w_own.shape[3]

    def f32(x):
        return x.astype(jnp.float32)

    def project(sender):
        rows = jnp.concatenate(
            [got[sender, :, r].reshape(wk.shape[0], NTOK) for r in range(cap)], axis=1
        )
        kv[sender, :, :, :cols] = (
            dot(rows, wk[...], 0, 0).astype(jnp.bfloat16).reshape(cap, NTOK, cols)
        )
        kv[sender, :, :, cols:] = (
            dot(rows, wv[...], 0, 0).astype(jnp.bfloat16).reshape(cap, NTOK, cols)
        )

    def weights_ready():
        for load in loads[:2]:
            load.wait()

    gather_sent = gather_steps(
        n, packed_hbm, got, local_sem, ga_sem, gy_sem, gs_sem, gf_sem, weights_ready, project
    )
    for load in loads[2:]:
        load.wait()

    def span(c):
        places = [(dev_ref[NEIGH * c + j], rank_ref[NEIGH * c + j]) for j in range(NEIGH)]
        keys = NEIGH * NTOK
        for j, (dev, rank) in enumerate(places):
            at = pl.ds(pl.multiple_of(c * keys + j * NTOK, NTOK), NTOK)
            blocks[:, :, :, at] = got[dev, :, rank].reshape(lines, 2, -1, NTOK)
        both = jnp.concatenate([kv[dev, rank] for dev, rank in places], axis=0)
        token_at = pl.ds(pl.multiple_of(c * CH, CH), CH)
        key_at = pl.ds(pl.multiple_of(c * keys, keys), keys)
        heads = [slice(h * DH, (h + 1) * DH) for h in range(cols // DH)]
        blank = jnp.zeros((CH, DH), jnp.bfloat16)
        corners = [
            jnp.concatenate(
                [
                    jnp.concatenate([q[token_at, at], blank], axis=1),
                    jnp.concatenate([blank, g[token_at, at]], axis=1),
                ],
                axis=0,
            )
            for at in heads
        ]
        scale = 1.0 / math.sqrt(DH)
        products = [
            dot(
                corner,
                jnp.concatenate([both[:, at], both[:, cols + at.start : cols + at.stop]], axis=1),
                1,
                1,
            )
            for corner, at in zip(corners, heads)
        ]
        scores = jnp.concatenate([product[:CH] for product in products], axis=0) * scale
        dprobs = jnp.concatenate([product[CH:] for product in products], axis=0)
        shifted = jnp.exp(scores - jnp.max(scores, axis=-1, keepdims=True))
        probs = shifted * (1.0 / jnp.sum(shifted, axis=-1, keepdims=True))
        delta = jnp.sum(probs * dprobs, axis=-1, keepdims=True)
        dscores = (probs * (dprobs - delta) * scale).astype(jnp.bfloat16)
        half = probs.astype(jnp.bfloat16)
        for h, at in enumerate(heads):
            rows = slice(h * CH, (h + 1) * CH)
            pair_rows = jnp.concatenate([dscores[rows], half[rows]], axis=0)
            grad = dot(pair_rows, corners[h], 0, 0).astype(jnp.bfloat16)
            grads[key_at, at] = grad[:, :DH]
            grads[key_at, cols + at.start : cols + at.stop] = grad[:, DH:]
            dq[token_at, at] = dot(dscores[rows], both[:, at], 1, 0).astype(jnp.bfloat16)

    def near_copy(out, landed, sems, i):
        return remote(out.at[i], landed.at[i], sems.at[0, i], sems.at[1, i], near)

    def far_copy(out, landed, sems, i):
        return remote(out.at[i], landed.at[i], sems.at[0, i], sems.at[1, i], far)

    def slot_terms(i):
        at = pl.ds(pl.multiple_of(i * s_cols, s_cols), s_cols)
        key_rows, value_rows = grads[at, :cols], grads[at, cols:]
        for part in range(2):
            for target, owner in ((s_out, 1 - low), (s_own, low)):
                rows = pl.ds(pl.multiple_of((2 * part + owner) * quarter, 16), quarter)
                term = dot(wk[rows, :], key_rows, 1, 1) + dot(wv[rows, :], value_rows, 1, 1)
                target[i, part] = term.astype(jnp.bfloat16)
        near_copy(s_out, s_in, ss_sem, i).start()

    def slot_pairs(i):
        near_copy(s_out, s_in, ss_sem, i).wait_recv()
        s_far[i] = (f32(s_own[i, 1 - high]) + f32(s_in[i, 1 - high])).astype(jnp.bfloat16)
        far_copy(s_far, s_far_in, sy_sem, i).start()

    def slot_sums(i):
        far_copy(s_far, s_far_in, sy_sem, i).wait_recv()
        total = (f32(s_own[i, high]) + f32(s_in[i, high]) + f32(s_far_in[i])).astype(jnp.bfloat16)
        per = s_cols // NTOK
        for j in range(per):
            s_sum[i * per + j] = total[:, j * NTOK : (j + 1) * NTOK]

    def query_terms(i):
        for part in range(2):
            for target, owner in ((q_out, 1 - low), (q_own, low)):
                start = (2 * part + owner) * (q_groups * q_cols) + i * q_cols
                rows = pl.ds(pl.multiple_of(start, q_cols), q_cols)
                target[i, part] = dot(dq[...], qw[rows, :], 1, 1).astype(jnp.bfloat16)
        near_copy(q_out, q_in, qs_sem, i).start()

    def query_pairs(i):
        near_copy(q_out, q_in, qs_sem, i).wait_recv()
        q_far[i] = (f32(q_own[i, 1 - high]) + f32(q_in[i, 1 - high])).astype(jnp.bfloat16)
        far_copy(q_far, q_far_in, qy_sem, i).start()

    def query_sums(i):
        far_copy(q_far, q_far_in, qy_sem, i).wait_recv()
        at = pl.ds(pl.multiple_of(i * q_cols, q_cols), q_cols)
        qi_ref[:, at] = (f32(q_own[i, high]) + f32(q_in[i, high]) + f32(q_far_in[i])).astype(
            jnp.bfloat16
        )

    def weight_dot(i, which):
        at = pl.ds(pl.multiple_of(i * w_cols, w_cols), w_cols)
        rows = blocks[:, which].reshape(lines * w_rows, blocks.shape[3])
        return dot(rows, grads[:, at], 1, 0).reshape(lines, w_rows, w_cols)

    def weight_copy(i):
        return remote(w_out.at[i], w_in.at[i], wx_sem.at[0, i], wx_sem.at[1, i], pair)

    def weight_send(i):
        w_out[i] = weight_dot(i, 1 - side).astype(jnp.bfloat16)
        weight_copy(i).start()

    def weight_keep(i):
        w_own[i] = weight_dot(i, side)

    def line_copy(i, k, sign):
        there = 2 * lax.rem(line + sign * k + lines, lines) + side
        return remote(
            w_far.at[i, k - 1],
            w_far_in.at[i, k - 1],
            wz_sem.at[0, i, k - 1],
            wz_sem.at[1, i, k - 1],
            {"dp": there},
        )

    def weight_pairs(i):
        weight_copy(i).wait_recv()
        for k in range(1, lines):
            there = lax.rem(line + k, lines)
            w_far[i, k - 1] = (w_own[i, there] + f32(w_in[i, there])).astype(jnp.bfloat16)
            line_copy(i, k, 1).start()

    def weight_sums(i):
        total = w_own[i, line] + f32(w_in[i, line])
        for k in range(1, lines):
            line_copy(i, k, -1).wait_recv()
            total = total + f32(w_far_in[i, k - 1])
        return total

    def back_copy(k):
        return remote(
            s_back.at[k - 1],
            s_back_in.at[k - 1],
            a_sem.at[0, k - 1],
            a_sem.at[1, k - 1],
            {"dp": lax.rem(me + k, n)},
        )

    def loop(start, count, body):
        def step(i, carry):
            body(i)
            return carry

        lax.fori_loop(start, count, step, 0)

    per_group = s_cols // (NEIGH * NTOK)

    def group(i):
        loop(i * per_group, (i + 1) * per_group, span)
        slot_terms(i)

    def group_step(i):
        group(i)
        slot_pairs(i - 1)

    group(0)
    loop(1, s_groups, group_step)
    weight_send(0)
    slot_pairs(s_groups - 1)
    loop(1, w_groups, weight_send)
    loop(0, s_groups, slot_sums)
    for k in range(1, n):
        there = lax.rem(me + k, n)
        for r in range(cap):
            s_back[k - 1, r] = s_sum[slot_ref[there * cap + r]]
        back_copy(k).start()
    for r in range(cap):
        ret_ref[me, r] = s_sum[slot_ref[me * cap + r]]

    def late_step(i):
        query_terms(i)
        weight_keep(i)
        weight_pairs(i)
        query_pairs(i)

    loop(0, q_groups, late_step)
    loop(0, q_groups, query_sums)
    for i in range(w_groups):
        total = weight_sums(i)
        at = i * w_cols
        out, at = (kw_ref, at) if at < cols else (vw_ref, at - cols)
        out[:, at : at + w_cols] = total
    for k in range(1, n):
        back_copy(k).wait_recv()
        ret_ref[lax.rem(me - k + n, n)] = s_back_in[k - 1]

    def sent(i):
        near_copy(s_out, s_in, ss_sem, i).wait_send()
        far_copy(s_far, s_far_in, sy_sem, i).wait_send()

    loop(0, s_groups, sent)

    def query_sent(i):
        near_copy(q_out, q_in, qs_sem, i).wait_send()
        far_copy(q_far, q_far_in, qy_sem, i).wait_send()

    loop(0, q_groups, query_sent)

    def weight_sent(i):
        weight_copy(i).wait_send()
        for k in range(1, lines):
            line_copy(i, k, 1).wait_send()

    loop(0, w_groups, weight_sent)
    for k in range(1, n):
        back_copy(k).wait_send()
    gather_sent()


def scatter_kernel(
    index_ref, ret_ref, qi_in, kw_in, vw_in, out_ref, qi_out, kw_out, vw_out, total, sems
):
    copies = [
        pltpu.make_async_copy(src, dst, sems.at[i])
        for i, (src, dst) in enumerate([(qi_in, qi_out), (kw_in, kw_out), (vw_in, vw_out)])
    ]
    for copy in copies:
        copy.start()
    total[...] = jnp.zeros_like(total)
    senders, cap = ret_ref.shape[:2]

    def add(i, carry):
        place = index_ref[i]

        @pl.when(place >= 0)
        def _():
            at = jnp.maximum(place, 0)
            total[at] += ret_ref[i // cap, i % cap].astype(jnp.float32)

        return carry

    lax.fori_loop(0, senders * cap, add, 0)

    def turn(i, carry):
        out_ref[i] = total[i].astype(jnp.bfloat16)
        return carry

    lax.fori_loop(0, total.shape[0], turn, 0)
    for copy in copies:
        copy.wait()


def call(kernel, out_shape, scratch, collective=None, **kwargs):
    params = dict(vmem_limit_bytes=VMEM_LIMIT)
    if collective is not None:
        params.update(collective_id=collective, has_side_effects=True)
    return pl.pallas_call(
        kernel,
        out_shape=out_shape,
        scratch_shapes=scratch,
        compiler_params=pltpu.CompilerParams(**params),
        **kwargs,
    )


def shards(
    queries,
    encodings,
    neighbour_ids,
    block_place,
    query_weight,
    key_weight,
    value_weight,
    attn_grad,
):
    n = lax.axis_size("dp")
    bf16, f32, i32 = jnp.bfloat16, jnp.float32, jnp.int32
    own_blocks, _, quarter = encodings.shape
    spans = neighbour_ids.shape[0]
    slots = spans * NEIGH
    cap = -(-slots // n)
    me = lax.axis_index("dp")
    cols = key_weight.shape[1]
    depth = key_weight.shape[0]
    vmem = pl.BlockSpec(memory_space=pltpu.VMEM)
    anywhere = pl.BlockSpec(memory_space=pl.ANY)
    dma = pltpu.SemaphoreType.DMA
    sds = jax.ShapeDtypeStruct

    position = block_place[neighbour_ids.reshape(-1)]
    padded = jnp.zeros((8, 128), i32).at[0, :slots].set(position)
    places = call(
        functools.partial(places_kernel, n),
        sds((n, 8, 128), i32),
        [pltpu.VMEM((n, 8, 128), i32), dma((n - 1,)), dma((n - 1,))],
        collective=0,
        in_specs=[vmem],
        out_specs=vmem,
    )(padded)[:, 0, :slots]

    earlier = jnp.arange(slots, dtype=i32)[None, :] < jnp.arange(slots, dtype=i32)[:, None]
    ranks = jnp.arange(cap, dtype=i32)
    mine = (places // own_blocks) == me
    asked_rank = jnp.sum((mine[:, None, :] & earlier[None]).astype(i32), axis=2)
    pick = mine[:, None, :] & (asked_rank[:, None, :] == ranks[None, :, None])
    asked = jnp.sum(jnp.where(pick, (places % own_blocks)[:, None, :] + 1, 0), axis=2) - 1
    owner = position // own_blocks
    rank = jnp.sum(((owner[:, None] == owner[None, :]) & earlier).astype(i32), axis=1)
    chosen = (owner[None, None, :] == jnp.arange(n, dtype=i32)[:, None, None]) & (
        rank[None, None, :] == ranks[None, :, None]
    )
    slot_at = jnp.sum(jnp.where(chosen, jnp.arange(slots, dtype=i32), 0), axis=2).reshape(-1)

    packed = jnp.swapaxes(encodings, 1, 2)[jnp.maximum(asked, 0)]
    tokens = slots * NTOK
    lines, w_rows, groups = n // 2, depth // n, 4
    s_cols = tokens // groups
    q_rows = queries.shape[0]
    q_width = query_weight.shape[0] // 4
    q_cols = q_width // groups
    w_cols = 2 * cols // groups

    def buffer(*shape, dtype=bf16):
        return pltpu.VMEM(shape, dtype)

    scratch = [
        buffer(n, 4, cap, quarter, NTOK),
        buffer(n, cap, NTOK, 2 * cols),
        buffer(lines, 2, w_rows, tokens),
        buffer(tokens, 2 * cols),
        buffer(q_rows, cols),
        buffer(q_rows, cols),
        buffer(q_rows, cols),
        buffer(*query_weight.shape),
        buffer(depth, cols),
        buffer(depth, cols),
        dma((5,)),
        dma,
        dma((2, n)),
        dma((2, n)),
        dma((2, n)),
        dma((2, n)),
        buffer(groups, 2, quarter, s_cols),
        buffer(groups, 2, quarter, s_cols),
        buffer(groups, 2, quarter, s_cols),
        buffer(groups, quarter, s_cols),
        buffer(groups, quarter, s_cols),
        buffer(slots, quarter, NTOK),
        buffer(n - 1, cap, quarter, NTOK),
        buffer(n - 1, cap, quarter, NTOK),
        buffer(groups, 2, q_rows, q_cols),
        buffer(groups, 2, q_rows, q_cols),
        buffer(groups, 2, q_rows, q_cols),
        buffer(groups, q_rows, q_cols),
        buffer(groups, q_rows, q_cols),
        buffer(groups, lines, w_rows, w_cols, dtype=f32),
        buffer(groups, lines, w_rows, w_cols),
        buffer(groups, lines, w_rows, w_cols),
        buffer(groups, lines - 1, w_rows, w_cols),
        buffer(groups, lines - 1, w_rows, w_cols),
        dma((2, groups)),
        dma((2, groups)),
        dma((2, n - 1)),
        dma((2, groups)),
        dma((2, groups)),
        dma((2, groups)),
        dma((2, groups, lines - 1)),
    ]
    query_input_grad, returned, key_grad, value_grad = call(
        functools.partial(exchange_kernel, n, cap),
        [
            sds((q_rows, q_width), bf16),
            sds((n, cap, quarter, NTOK), bf16),
            sds((w_rows, cols), f32),
            sds((w_rows, cols), f32),
        ],
        scratch,
        collective=1,
        in_specs=[pl.BlockSpec(memory_space=pltpu.SMEM)] * 3 + [anywhere] * 6,
        out_specs=[vmem] * 4,
    )(
        owner,
        rank,
        slot_at,
        packed,
        queries,
        attn_grad,
        query_weight,
        key_weight,
        value_weight,
    )
    encodings_grad, query_input_grad, key_grad, value_grad = call(
        scatter_kernel,
        [
            sds((own_blocks, quarter, NTOK), bf16),
            sds(query_input_grad.shape, bf16),
            sds(key_grad.shape, f32),
            sds(value_grad.shape, f32),
        ],
        [pltpu.VMEM((own_blocks, quarter, NTOK), f32), dma((3,))],
        in_specs=[pl.BlockSpec(memory_space=pltpu.SMEM), vmem] + [anywhere] * 3,
        out_specs=[vmem] + [anywhere] * 3,
    )(asked.reshape(-1), returned, query_input_grad, key_grad, value_grad)
    return query_input_grad, jnp.swapaxes(encodings_grad, 1, 2), key_grad, value_grad


def fits(mesh):
    dp, head = mesh.shape["dp"], mesh.shape["head"]
    return head == 4 and dp % 2 == 0 and dp > 2 and E % (16 * dp) == 0


def solution(mesh):
    in_specs = (
        P("dp", "head"),
        P("dp", None, "head"),
        P("dp", None),
        P(),
        P(None, "head"),
        P(None, "head"),
        P(None, "head"),
        P("dp", "head"),
    )
    out_specs = (P("dp", "head"), P("dp", None, "head"), P("dp", "head"), P("dp", "head"))
    return jax.shard_map(
        shards if fits(mesh) else plain_shards,
        mesh=mesh,
        in_specs=in_specs,
        out_specs=out_specs,
        check_vma=False,
    )
```

```python
import functools
import math

import jax
import jax.numpy as jnp
from jax import lax
from jax.experimental import pallas as pl
from jax.experimental.pallas import tpu as pltpu
from jax.sharding import PartitionSpec as P

DH = 128
E = 896
CH = 64
NTOK = 128
NEIGH = 2


def plain_shards(
    queries,
    encodings,
    neighbour_ids,
    block_place,
    query_weight,
    key_weight,
    value_weight,
    attn_grad,
):
    dp_count = lax.axis_size("dp")
    own_blocks = encodings.shape[0]
    span_count = neighbour_ids.shape[0]
    block_names = neighbour_ids.reshape(-1)
    slot_count = block_names.shape[0]
    capacity = -(-slot_count // dp_count)
    position = block_place[block_names]
    owner_dev = position // own_blocks
    local_slot = position % own_blocks
    slot_order = jnp.arange(slot_count, dtype=jnp.int32)
    same_owner = (owner_dev[:, None] == owner_dev[None, :]) & (
        slot_order[None, :] < slot_order[:, None]
    )
    slot_rank = jnp.sum(same_owner.astype(jnp.int32), axis=1)
    device_match = owner_dev[:, None, None] == jnp.arange(dp_count, dtype=jnp.int32)[None, :, None]
    rank_match = slot_rank[:, None, None] == jnp.arange(capacity, dtype=jnp.int32)[None, None, :]
    requests = (
        jnp.sum(jnp.where(device_match & rank_match, local_slot[:, None, None] + 1, 0), axis=0) - 1
    )
    asked_rows = lax.all_to_all(requests, "dp", split_axis=0, concat_axis=0, tiled=True)
    valid_mask = asked_rows >= 0
    local_index = jnp.maximum(asked_rows, 0)
    blank = jnp.zeros((), jnp.bfloat16)
    packed = jnp.where(valid_mask[:, :, None, None], encodings[local_index], blank)
    received = lax.all_to_all(packed, "dp", split_axis=0, concat_axis=0, tiled=True)
    slot_blocks = lax.all_gather(received[owner_dev, slot_rank], "head", axis=2, tiled=True)
    flat_rows = slot_blocks.reshape(-1, E)
    both_weights = jnp.concatenate([key_weight, value_weight], axis=1)
    head_cols = key_weight.shape[1]
    local_heads = head_cols // DH
    projected = jnp.dot(flat_rows, both_weights, preferred_element_type=jnp.float32).astype(
        jnp.bfloat16
    )
    key_rows = projected[:, :head_cols].reshape(span_count, NEIGH * NTOK, local_heads, DH)
    value_rows = projected[:, head_cols:].reshape(span_count, NEIGH * NTOK, local_heads, DH)
    query_heads = queries.reshape(span_count, CH, local_heads, DH)
    grad_heads = attn_grad.reshape(span_count, CH, local_heads, DH)
    score_scale = 1.0 / math.sqrt(DH)
    scores = (
        jnp.einsum("cqhd,ckhd->chqk", query_heads, key_rows, preferred_element_type=jnp.float32)
        * score_scale
    )
    shifted = jnp.exp(scores - jnp.max(scores, axis=-1, keepdims=True))
    prob_rows = shifted / jnp.sum(shifted, axis=-1, keepdims=True)
    prob_half = prob_rows.astype(jnp.bfloat16)
    grad_probs = jnp.einsum(
        "cqhd,ckhd->chqk", grad_heads, value_rows, preferred_element_type=jnp.float32
    )
    row_delta = jnp.sum(prob_rows * grad_probs, axis=-1, keepdims=True)
    grad_scores = (prob_rows * (grad_probs - row_delta) * score_scale).astype(jnp.bfloat16)
    value_grad = jnp.einsum(
        "chqk,cqhd->ckhd", prob_half, grad_heads, preferred_element_type=jnp.float32
    ).astype(jnp.bfloat16)
    key_grad = jnp.einsum(
        "chqk,cqhd->ckhd", grad_scores, query_heads, preferred_element_type=jnp.float32
    ).astype(jnp.bfloat16)
    query_grad = jnp.einsum(
        "chqk,ckhd->cqhd", grad_scores, key_rows, preferred_element_type=jnp.float32
    ).astype(jnp.bfloat16)
    partial_input = jnp.dot(
        query_grad.reshape(-1, head_cols), query_weight.T, preferred_element_type=jnp.float32
    )
    query_input_grad = lax.psum_scatter(
        partial_input.astype(jnp.bfloat16), "head", scatter_dimension=1, tiled=True
    )
    both_grads = jnp.concatenate(
        [key_grad.reshape(-1, head_cols), value_grad.reshape(-1, head_cols)], axis=1
    )
    weight_grads = lax.psum_scatter(
        lax.dot_general(
            flat_rows, both_grads, (((0,), (0,)), ((), ())), preferred_element_type=jnp.float32
        ),
        "dp",
        scatter_dimension=0,
        tiled=True,
    )
    slot_partial = jnp.dot(both_grads, both_weights.T, preferred_element_type=jnp.float32).reshape(
        slot_count, NTOK, E
    )
    slot_grad = lax.psum_scatter(
        slot_partial.astype(jnp.bfloat16), "head", scatter_dimension=2, tiled=True
    )
    quarter = slot_grad.shape[2]
    outgoing = (
        jnp.zeros((dp_count, capacity, NTOK, quarter), jnp.bfloat16)
        .at[owner_dev, slot_rank]
        .set(slot_grad)
    )
    returned = lax.all_to_all(outgoing, "dp", split_axis=0, concat_axis=0, tiled=True)
    block_match = (
        local_index.reshape(-1)[None, :] == jnp.arange(own_blocks, dtype=jnp.int32)[:, None]
    )
    target = (block_match & valid_mask.reshape(-1)[None, :]).astype(jnp.bfloat16)
    encodings_grad = jnp.dot(
        target, returned.reshape(dp_count * capacity, -1), preferred_element_type=jnp.float32
    )
    encodings_grad = encodings_grad.reshape(own_blocks, NTOK, quarter).astype(jnp.bfloat16)
    return (
        query_input_grad,
        encodings_grad,
        weight_grads[:, :head_cols],
        weight_grads[:, head_cols:],
    )

MESH = pl.DeviceIdType.MESH
VMEM_LIMIT = 60 * 1024 * 1024


def remote(src, dst, send_sem, recv_sem, device):
    return pltpu.make_async_remote_copy(
        src_ref=src,
        dst_ref=dst,
        send_sem=send_sem,
        recv_sem=recv_sem,
        device_id=device,
        device_id_type=MESH,
    )


def greet(devices):
    barrier = pltpu.get_barrier_semaphore()
    for device in devices:
        pl.semaphore_signal(barrier, inc=1, device_id=device, device_id_type=MESH)
    pl.semaphore_wait(barrier, len(devices))


def places_kernel(n, mine_ref, all_ref, landed, send_sem, recv_sem):
    me = lax.axis_index("dp")
    greet([{"dp": lax.rem(me + k, n)} for k in range(1, n)])
    copies = []
    for k in range(1, n):
        copy = remote(
            mine_ref,
            landed.at[me],
            send_sem.at[k - 1],
            recv_sem.at[k - 1],
            {"dp": lax.rem(me + k, n)},
        )
        copy.start()
        copies.append(copy)
    for k in range(1, n):
        sender = lax.rem(me - k + n, n)
        remote(
            mine_ref, landed.at[sender], send_sem.at[k - 1], recv_sem.at[k - 1], {"dp": sender}
        ).wait_recv()
        all_ref[sender] = landed[sender]
    all_ref[me] = mine_ref[...]
    for copy in copies:
        copy.wait_send()


def gather_steps(n, packed, got, local_sem, a_sem, y_sem, s_sem, f_sem, ready, project):
    me = lax.axis_index("dp")
    col = lax.axis_index("head")
    far = lax.rem(col + 2, 4)
    near = col + 1 - 2 * lax.rem(col, 2)
    far_near = lax.rem(near + 2, 4)
    ahead = 3

    def first(k):
        there = lax.rem(me + k, n)
        return remote(
            packed.at[there], got.at[me, col], a_sem.at[0, k], a_sem.at[1, k], {"dp": there}
        )

    def arrived(k):
        sender = lax.rem(me - k + n, n)
        return remote(
            packed.at[sender], got.at[sender, col], a_sem.at[0, k], a_sem.at[1, k], {"dp": sender}
        )

    def across(k, feature, sems, target):
        block = got.at[lax.rem(me - k + n, n), feature]
        return remote(block, block, sems.at[0, k], sems.at[1, k], {"head": target})

    own = pltpu.make_async_copy(packed.at[me], got.at[me, col], local_sem)
    own.start()
    for k in range(1, min(n, 1 + ahead)):
        first(k).start()
    own.wait()

    def spread(k):
        across(k, col, y_sem, far).start()
        across(k, col, s_sem, near).start()

    def pass_on(k):
        across(k, far, y_sem, far).wait_recv()
        across(k, far, f_sem, near).start()

    def take(k):
        across(k, near, s_sem, near).wait_recv()
        across(k, far_near, f_sem, near).wait_recv()
        project(lax.rem(me - k + n, n))

    spread(0)
    for k in range(1, n):
        arrived(k).wait_recv()
        spread(k)
        if k + ahead < n:
            first(k + ahead).start()
    pass_on(0)
    ready()

    def step(k, carry):
        pass_on(k)
        take(k - 1)
        return carry

    lax.fori_loop(1, n, step, 0)
    take(n - 1)

    def finish():
        for k in range(n):
            if k:
                first(k).wait_send()
            across(k, col, y_sem, far).wait_send()
            across(k, col, s_sem, near).wait_send()
            across(k, far, f_sem, near).wait_send()

    return finish


def dot(a, b, over_a, over_b):
    return lax.dot_general(
        a, b, (((over_a,), (over_b,)), ((), ())), preferred_element_type=jnp.float32
    )


def exchange_kernel(
    n,
    cap,
    dev_ref,
    rank_ref,
    slot_ref,
    packed_ref,
    q_hbm,
    g_hbm,
    qw_hbm,
    wk_hbm,
    wv_hbm,
    qi_ref,
    ret_ref,
    kw_ref,
    vw_ref,
    got,
    kv,
    blocks,
    grads,
    dq,
    q,
    g,
    qw,
    wk,
    wv,
    load_sem,
    local_sem,
    ga_sem,
    gy_sem,
    gs_sem,
    gf_sem,
    s_own,
    s_out,
    s_in,
    s_far,
    s_far_in,
    s_sum,
    s_back,
    s_back_in,
    q_own,
    q_out,
    q_in,
    q_far,
    q_far_in,
    w_own,
    w_out,
    w_in,
    w_far,
    w_far_in,
    ss_sem,
    sy_sem,
    a_sem,
    qs_sem,
    qy_sem,
    wx_sem,
    wz_sem,
):
    me = lax.axis_index("dp")
    col = lax.axis_index("head")
    high, low = col // 2, lax.rem(col, 2)
    far = {"head": lax.rem(col + 2, 4)}
    near = {"head": col + 1 - 2 * low}
    side, line = lax.rem(me, 2), me // 2
    lines = n // 2
    pair = {"dp": me + 1 - 2 * side}
    loads = [
        pltpu.make_async_copy(src, dst, load_sem.at[i])
        for i, (src, dst) in enumerate(
            [
                (wk_hbm, wk),
                (wv_hbm, wv),
                (q_hbm, q),
                (g_hbm, g),
                (qw_hbm, qw),
            ]
        )
    ]
    for load in loads:
        load.start()
    greet([{"dp": lax.rem(me + k, n)} for k in range(1, n)] + [far, near])
    s_groups, quarter, s_cols = s_far.shape
    cols = wk.shape[1]
    q_groups, q_rows, q_cols = q_far.shape
    w_groups, w_rows, w_cols = w_own.shape[0], w_own.shape[2], w_own.shape[3]

    def f32(x):
        return x.astype(jnp.float32)

    def project(sender):
        rows = jnp.concatenate(
            [got[sender, :, r].reshape(wk.shape[0], NTOK) for r in range(cap)], axis=1
        )
        kv[sender, :, :, :cols] = (
            dot(rows, wk[...], 0, 0).astype(jnp.bfloat16).reshape(cap, NTOK, cols)
        )
        kv[sender, :, :, cols:] = (
            dot(rows, wv[...], 0, 0).astype(jnp.bfloat16).reshape(cap, NTOK, cols)
        )

    def weights_ready():
        for load in loads[:2]:
            load.wait()

    gather_sent = gather_steps(
        n, packed_ref, got, local_sem, ga_sem, gy_sem, gs_sem, gf_sem, weights_ready, project
    )
    for load in loads[2:]:
        load.wait()

    def span(c):
        places = [(dev_ref[NEIGH * c + j], rank_ref[NEIGH * c + j]) for j in range(NEIGH)]
        keys = NEIGH * NTOK
        for j, (dev, rank) in enumerate(places):
            at = pl.ds(pl.multiple_of(c * keys + j * NTOK, NTOK), NTOK)
            blocks[:, :, :, at] = got[dev, :, rank].reshape(lines, 2, -1, NTOK)
        both = jnp.concatenate([kv[dev, rank] for dev, rank in places], axis=0)
        token_at = pl.ds(pl.multiple_of(c * CH, CH), CH)
        key_at = pl.ds(pl.multiple_of(c * keys, keys), keys)
        heads = [slice(h * DH, (h + 1) * DH) for h in range(cols // DH)]
        blank = jnp.zeros((CH, DH), jnp.bfloat16)
        corners = [
            jnp.concatenate(
                [
                    jnp.concatenate([q[token_at, at], blank], axis=1),
                    jnp.concatenate([blank, g[token_at, at]], axis=1),
                ],
                axis=0,
            )
            for at in heads
        ]
        scale = 1.0 / math.sqrt(DH)
        products = [
            dot(
                corner,
                jnp.concatenate([both[:, at], both[:, cols + at.start : cols + at.stop]], axis=1),
                1,
                1,
            )
            for corner, at in zip(corners, heads)
        ]
        scores = jnp.concatenate([product[:CH] for product in products], axis=0) * scale
        dprobs = jnp.concatenate([product[CH:] for product in products], axis=0)
        shifted = jnp.exp(scores - jnp.max(scores, axis=-1, keepdims=True))
        probs = shifted * (1.0 / jnp.sum(shifted, axis=-1, keepdims=True))
        delta = jnp.sum(probs * dprobs, axis=-1, keepdims=True)
        dscores = (probs * (dprobs - delta) * scale).astype(jnp.bfloat16)
        half = probs.astype(jnp.bfloat16)
        for h, at in enumerate(heads):
            rows = slice(h * CH, (h + 1) * CH)
            pair_rows = jnp.concatenate([dscores[rows], half[rows]], axis=0)
            grad = dot(pair_rows, corners[h], 0, 0).astype(jnp.bfloat16)
            grads[key_at, at] = grad[:, :DH]
            grads[key_at, cols + at.start : cols + at.stop] = grad[:, DH:]
            dq[token_at, at] = dot(dscores[rows], both[:, at], 1, 0).astype(jnp.bfloat16)

    def near_copy(out, landed, sems, i):
        return remote(out.at[i], landed.at[i], sems.at[0, i], sems.at[1, i], near)

    def far_copy(out, landed, sems, i):
        return remote(out.at[i], landed.at[i], sems.at[0, i], sems.at[1, i], far)

    def slot_terms(i):
        at = pl.ds(pl.multiple_of(i * s_cols, s_cols), s_cols)
        key_rows, value_rows = grads[at, :cols], grads[at, cols:]
        for part in range(2):
            for target, owner in ((s_out, 1 - low), (s_own, low)):
                rows = pl.ds(pl.multiple_of((2 * part + owner) * quarter, 16), quarter)
                term = dot(wk[rows, :], key_rows, 1, 1) + dot(wv[rows, :], value_rows, 1, 1)
                target[i, part] = term.astype(jnp.bfloat16)
        near_copy(s_out, s_in, ss_sem, i).start()

    def slot_pairs(i):
        near_copy(s_out, s_in, ss_sem, i).wait_recv()
        s_far[i] = (f32(s_own[i, 1 - high]) + f32(s_in[i, 1 - high])).astype(jnp.bfloat16)
        far_copy(s_far, s_far_in, sy_sem, i).start()

    def slot_sums(i):
        far_copy(s_far, s_far_in, sy_sem, i).wait_recv()
        total = (f32(s_own[i, high]) + f32(s_in[i, high]) + f32(s_far_in[i])).astype(jnp.bfloat16)
        per = s_cols // NTOK
        for j in range(per):
            s_sum[i * per + j] = total[:, j * NTOK : (j + 1) * NTOK]

    def query_terms(i):
        for part in range(2):
            for target, owner in ((q_out, 1 - low), (q_own, low)):
                start = (2 * part + owner) * (q_groups * q_cols) + i * q_cols
                rows = pl.ds(pl.multiple_of(start, q_cols), q_cols)
                target[i, part] = dot(dq[...], qw[rows, :], 1, 1).astype(jnp.bfloat16)
        near_copy(q_out, q_in, qs_sem, i).start()

    def query_pairs(i):
        near_copy(q_out, q_in, qs_sem, i).wait_recv()
        q_far[i] = (f32(q_own[i, 1 - high]) + f32(q_in[i, 1 - high])).astype(jnp.bfloat16)
        far_copy(q_far, q_far_in, qy_sem, i).start()

    def query_sums(i):
        far_copy(q_far, q_far_in, qy_sem, i).wait_recv()
        at = pl.ds(pl.multiple_of(i * q_cols, q_cols), q_cols)
        qi_ref[:, at] = (f32(q_own[i, high]) + f32(q_in[i, high]) + f32(q_far_in[i])).astype(
            jnp.bfloat16
        )

    def weight_dot(i, which):
        at = pl.ds(pl.multiple_of(i * w_cols, w_cols), w_cols)
        rows = blocks[:, which].reshape(lines * w_rows, blocks.shape[3])
        return dot(rows, grads[:, at], 1, 0).reshape(lines, w_rows, w_cols)

    def weight_copy(i):
        return remote(w_out.at[i], w_in.at[i], wx_sem.at[0, i], wx_sem.at[1, i], pair)

    def weight_send(i):
        w_out[i] = weight_dot(i, 1 - side).astype(jnp.bfloat16)
        weight_copy(i).start()

    def weight_keep(i):
        w_own[i] = weight_dot(i, side)

    def line_copy(i, k, sign):
        there = 2 * lax.rem(line + sign * k + lines, lines) + side
        return remote(
            w_far.at[i, k - 1],
            w_far_in.at[i, k - 1],
            wz_sem.at[0, i, k - 1],
            wz_sem.at[1, i, k - 1],
            {"dp": there},
        )

    def weight_pairs(i):
        weight_copy(i).wait_recv()
        for k in range(1, lines):
            there = lax.rem(line + k, lines)
            w_far[i, k - 1] = (w_own[i, there] + f32(w_in[i, there])).astype(jnp.bfloat16)
            line_copy(i, k, 1).start()

    def weight_sums(i):
        total = w_own[i, line] + f32(w_in[i, line])
        for k in range(1, lines):
            line_copy(i, k, -1).wait_recv()
            total = total + f32(w_far_in[i, k - 1])
        return total

    def back_copy(k):
        return remote(
            s_back.at[k - 1],
            s_back_in.at[k - 1],
            a_sem.at[0, k - 1],
            a_sem.at[1, k - 1],
            {"dp": lax.rem(me + k, n)},
        )

    def loop(start, count, body):
        def step(i, carry):
            body(i)
            return carry

        lax.fori_loop(start, count, step, 0)

    per_group = s_cols // (NEIGH * NTOK)

    def group(i):
        loop(i * per_group, (i + 1) * per_group, span)
        slot_terms(i)

    def group_step(i):
        group(i)
        slot_pairs(i - 1)

    group(0)
    loop(1, s_groups, group_step)
    weight_send(0)
    slot_pairs(s_groups - 1)
    early = q_groups // 2

    def early_step(i):
        query_terms(i)
        weight_send(i + 1)
        query_pairs(i)

    loop(0, early, early_step)
    loop(early + 1, w_groups, weight_send)
    loop(0, s_groups, slot_sums)
    for k in range(1, n):
        there = lax.rem(me + k, n)
        for r in range(cap):
            s_back[k - 1, r] = s_sum[slot_ref[there * cap + r]]
        back_copy(k).start()
    for r in range(cap):
        ret_ref[me, r] = s_sum[slot_ref[me * cap + r]]

    def late_step(i):
        query_terms(early + i)
        weight_keep(i)
        weight_pairs(i)
        query_pairs(early + i)

    loop(0, q_groups - early, late_step)

    def last_step(i):
        weight_keep(i)
        weight_pairs(i)

    loop(q_groups - early, w_groups, last_step)
    loop(0, q_groups, query_sums)
    for i in range(w_groups):
        total = weight_sums(i)
        at = i * w_cols
        out, at = (kw_ref, at) if at < cols else (vw_ref, at - cols)
        out[:, at : at + w_cols] = total
    for k in range(1, n):
        back_copy(k).wait_recv()
        ret_ref[lax.rem(me - k + n, n)] = s_back_in[k - 1]

    def sent(i):
        near_copy(s_out, s_in, ss_sem, i).wait_send()
        far_copy(s_far, s_far_in, sy_sem, i).wait_send()

    loop(0, s_groups, sent)

    def query_sent(i):
        near_copy(q_out, q_in, qs_sem, i).wait_send()
        far_copy(q_far, q_far_in, qy_sem, i).wait_send()

    loop(0, q_groups, query_sent)

    def weight_sent(i):
        weight_copy(i).wait_send()
        for k in range(1, lines):
            line_copy(i, k, 1).wait_send()

    loop(0, w_groups, weight_sent)
    for k in range(1, n):
        back_copy(k).wait_send()
    gather_sent()


def scatter_kernel(
    index_ref, ret_ref, qi_in, kw_in, vw_in, out_ref, qi_out, kw_out, vw_out, total
):
    qi_out[...] = qi_in[...]
    kw_out[...] = kw_in[...]
    vw_out[...] = vw_in[...]
    total[...] = jnp.zeros_like(total)
    senders, cap = ret_ref.shape[:2]

    def add(i, carry):
        place = index_ref[i]

        @pl.when(place >= 0)
        def _():
            at = jnp.maximum(place, 0)
            total[at] += ret_ref[i // cap, i % cap].astype(jnp.float32)

        return carry

    lax.fori_loop(0, senders * cap, add, 0)

    def turn(i, carry):
        out_ref[i] = total[i].astype(jnp.bfloat16)
        return carry

    lax.fori_loop(0, total.shape[0], turn, 0)


def call(kernel, out_shape, scratch, collective=None, **kwargs):
    params = dict(vmem_limit_bytes=VMEM_LIMIT)
    if collective is not None:
        params.update(collective_id=collective, has_side_effects=True)
    return pl.pallas_call(
        kernel,
        out_shape=out_shape,
        scratch_shapes=scratch,
        compiler_params=pltpu.CompilerParams(**params),
        **kwargs,
    )


def shards(
    queries,
    encodings,
    neighbour_ids,
    block_place,
    query_weight,
    key_weight,
    value_weight,
    attn_grad,
):
    n = lax.axis_size("dp")
    bf16, f32, i32 = jnp.bfloat16, jnp.float32, jnp.int32
    own_blocks, _, quarter = encodings.shape
    spans = neighbour_ids.shape[0]
    slots = spans * NEIGH
    cap = -(-slots // n)
    me = lax.axis_index("dp")
    cols = key_weight.shape[1]
    depth = key_weight.shape[0]
    vmem = pl.BlockSpec(memory_space=pltpu.VMEM)
    anywhere = pl.BlockSpec(memory_space=pl.ANY)
    dma = pltpu.SemaphoreType.DMA
    sds = jax.ShapeDtypeStruct

    position = block_place[neighbour_ids.reshape(-1)]
    padded = jnp.zeros((8, 128), i32).at[0, :slots].set(position)
    places = call(
        functools.partial(places_kernel, n),
        sds((n, 8, 128), i32),
        [pltpu.VMEM((n, 8, 128), i32), dma((n - 1,)), dma((n - 1,))],
        collective=0,
        in_specs=[vmem],
        out_specs=vmem,
    )(padded)[:, 0, :slots]

    earlier = jnp.arange(slots, dtype=i32)[None, :] < jnp.arange(slots, dtype=i32)[:, None]
    ranks = jnp.arange(cap, dtype=i32)
    mine = (places // own_blocks) == me
    asked_rank = jnp.sum((mine[:, None, :] & earlier[None]).astype(i32), axis=2)
    pick = mine[:, None, :] & (asked_rank[:, None, :] == ranks[None, :, None])
    asked = jnp.sum(jnp.where(pick, (places % own_blocks)[:, None, :] + 1, 0), axis=2) - 1
    owner = position // own_blocks
    rank = jnp.sum(((owner[:, None] == owner[None, :]) & earlier).astype(i32), axis=1)
    chosen = (owner[None, None, :] == jnp.arange(n, dtype=i32)[:, None, None]) & (
        rank[None, None, :] == ranks[None, :, None]
    )
    slot_at = jnp.sum(jnp.where(chosen, jnp.arange(slots, dtype=i32), 0), axis=2).reshape(-1)

    packed = jnp.swapaxes(encodings, 1, 2)[jnp.maximum(asked, 0)]
    tokens = slots * NTOK
    lines, w_rows, groups = n // 2, depth // n, 4
    s_cols = tokens // groups
    q_rows = queries.shape[0]
    q_width = query_weight.shape[0] // 4
    q_cols = q_width // groups
    w_cols = 2 * cols // groups

    def buffer(*shape, dtype=bf16):
        return pltpu.VMEM(shape, dtype)

    scratch = [
        buffer(n, 4, cap, quarter, NTOK),
        buffer(n, cap, NTOK, 2 * cols),
        buffer(lines, 2, w_rows, tokens),
        buffer(tokens, 2 * cols),
        buffer(q_rows, cols),
        buffer(q_rows, cols),
        buffer(q_rows, cols),
        buffer(*query_weight.shape),
        buffer(depth, cols),
        buffer(depth, cols),
        dma((5,)),
        dma,
        dma((2, n)),
        dma((2, n)),
        dma((2, n)),
        dma((2, n)),
        buffer(groups, 2, quarter, s_cols),
        buffer(groups, 2, quarter, s_cols),
        buffer(groups, 2, quarter, s_cols),
        buffer(groups, quarter, s_cols),
        buffer(groups, quarter, s_cols),
        buffer(slots, quarter, NTOK),
        buffer(n - 1, cap, quarter, NTOK),
        buffer(n - 1, cap, quarter, NTOK),
        buffer(groups, 2, q_rows, q_cols),
        buffer(groups, 2, q_rows, q_cols),
        buffer(groups, 2, q_rows, q_cols),
        buffer(groups, q_rows, q_cols),
        buffer(groups, q_rows, q_cols),
        buffer(groups, lines, w_rows, w_cols, dtype=f32),
        buffer(groups, lines, w_rows, w_cols),
        buffer(groups, lines, w_rows, w_cols),
        buffer(groups, lines - 1, w_rows, w_cols),
        buffer(groups, lines - 1, w_rows, w_cols),
        dma((2, groups)),
        dma((2, groups)),
        dma((2, n - 1)),
        dma((2, groups)),
        dma((2, groups)),
        dma((2, groups)),
        dma((2, groups, lines - 1)),
    ]
    query_input_grad, returned, key_grad, value_grad = call(
        functools.partial(exchange_kernel, n, cap),
        [
            sds((q_rows, q_width), bf16),
            sds((n, cap, quarter, NTOK), bf16),
            sds((w_rows, cols), f32),
            sds((w_rows, cols), f32),
        ],
        scratch,
        collective=1,
        in_specs=[pl.BlockSpec(memory_space=pltpu.SMEM)] * 3 + [vmem] + [anywhere] * 5,
        out_specs=[vmem] * 4,
    )(
        owner,
        rank,
        slot_at,
        packed,
        queries,
        attn_grad,
        query_weight,
        key_weight,
        value_weight,
    )
    encodings_grad, query_input_grad, key_grad, value_grad = call(
        scatter_kernel,
        [
            sds((own_blocks, quarter, NTOK), bf16),
            sds(query_input_grad.shape, bf16),
            sds(key_grad.shape, f32),
            sds(value_grad.shape, f32),
        ],
        [pltpu.VMEM((own_blocks, quarter, NTOK), f32)],
        in_specs=[pl.BlockSpec(memory_space=pltpu.SMEM), vmem, vmem, vmem, vmem],
        out_specs=[vmem] * 4,
    )(asked.reshape(-1), returned, query_input_grad, key_grad, value_grad)
    return query_input_grad, jnp.swapaxes(encodings_grad, 1, 2), key_grad, value_grad


def fits(mesh):
    dp, head = mesh.shape["dp"], mesh.shape["head"]
    return head == 4 and dp % 2 == 0 and dp > 2 and E % (16 * dp) == 0


def solution(mesh):
    in_specs = (
        P("dp", "head"),
        P("dp", None, "head"),
        P("dp", None),
        P(),
        P(None, "head"),
        P(None, "head"),
        P(None, "head"),
        P("dp", "head"),
    )
    out_specs = (P("dp", "head"), P("dp", None, "head"), P("dp", "head"), P("dp", "head"))
    return jax.shard_map(
        shards if fits(mesh) else plain_shards,
        mesh=mesh,
        in_specs=in_specs,
        out_specs=out_specs,
        check_vma=False,
    )
```

```python
import functools
import math

import jax
import jax.numpy as jnp
from jax import lax
from jax.experimental import pallas as pl
from jax.experimental.pallas import tpu as pltpu
from jax.sharding import PartitionSpec as P

DH = 128
E = 896
CH = 64
NTOK = 128
NEIGH = 2


def plain_shards(
    queries,
    encodings,
    neighbour_ids,
    block_place,
    query_weight,
    key_weight,
    value_weight,
    attn_grad,
):
    dp_count = lax.axis_size("dp")
    own_blocks = encodings.shape[0]
    span_count = neighbour_ids.shape[0]
    block_names = neighbour_ids.reshape(-1)
    slot_count = block_names.shape[0]
    capacity = -(-slot_count // dp_count)
    position = block_place[block_names]
    owner_dev = position // own_blocks
    local_slot = position % own_blocks
    slot_order = jnp.arange(slot_count, dtype=jnp.int32)
    same_owner = (owner_dev[:, None] == owner_dev[None, :]) & (
        slot_order[None, :] < slot_order[:, None]
    )
    slot_rank = jnp.sum(same_owner.astype(jnp.int32), axis=1)
    device_match = owner_dev[:, None, None] == jnp.arange(dp_count, dtype=jnp.int32)[None, :, None]
    rank_match = slot_rank[:, None, None] == jnp.arange(capacity, dtype=jnp.int32)[None, None, :]
    requests = (
        jnp.sum(jnp.where(device_match & rank_match, local_slot[:, None, None] + 1, 0), axis=0) - 1
    )
    asked_rows = lax.all_to_all(requests, "dp", split_axis=0, concat_axis=0, tiled=True)
    valid_mask = asked_rows >= 0
    local_index = jnp.maximum(asked_rows, 0)
    blank = jnp.zeros((), jnp.bfloat16)
    packed = jnp.where(valid_mask[:, :, None, None], encodings[local_index], blank)
    received = lax.all_to_all(packed, "dp", split_axis=0, concat_axis=0, tiled=True)
    slot_blocks = lax.all_gather(received[owner_dev, slot_rank], "head", axis=2, tiled=True)
    flat_rows = slot_blocks.reshape(-1, E)
    both_weights = jnp.concatenate([key_weight, value_weight], axis=1)
    head_cols = key_weight.shape[1]
    local_heads = head_cols // DH
    projected = jnp.dot(flat_rows, both_weights, preferred_element_type=jnp.float32).astype(
        jnp.bfloat16
    )
    key_rows = projected[:, :head_cols].reshape(span_count, NEIGH * NTOK, local_heads, DH)
    value_rows = projected[:, head_cols:].reshape(span_count, NEIGH * NTOK, local_heads, DH)
    query_heads = queries.reshape(span_count, CH, local_heads, DH)
    grad_heads = attn_grad.reshape(span_count, CH, local_heads, DH)
    score_scale = 1.0 / math.sqrt(DH)
    scores = (
        jnp.einsum("cqhd,ckhd->chqk", query_heads, key_rows, preferred_element_type=jnp.float32)
        * score_scale
    )
    shifted = jnp.exp(scores - jnp.max(scores, axis=-1, keepdims=True))
    prob_rows = shifted / jnp.sum(shifted, axis=-1, keepdims=True)
    prob_half = prob_rows.astype(jnp.bfloat16)
    grad_probs = jnp.einsum(
        "cqhd,ckhd->chqk", grad_heads, value_rows, preferred_element_type=jnp.float32
    )
    row_delta = jnp.sum(prob_rows * grad_probs, axis=-1, keepdims=True)
    grad_scores = (prob_rows * (grad_probs - row_delta) * score_scale).astype(jnp.bfloat16)
    value_grad = jnp.einsum(
        "chqk,cqhd->ckhd", prob_half, grad_heads, preferred_element_type=jnp.float32
    ).astype(jnp.bfloat16)
    key_grad = jnp.einsum(
        "chqk,cqhd->ckhd", grad_scores, query_heads, preferred_element_type=jnp.float32
    ).astype(jnp.bfloat16)
    query_grad = jnp.einsum(
        "chqk,ckhd->cqhd", grad_scores, key_rows, preferred_element_type=jnp.float32
    ).astype(jnp.bfloat16)
    partial_input = jnp.dot(
        query_grad.reshape(-1, head_cols), query_weight.T, preferred_element_type=jnp.float32
    )
    query_input_grad = lax.psum_scatter(
        partial_input.astype(jnp.bfloat16), "head", scatter_dimension=1, tiled=True
    )
    both_grads = jnp.concatenate(
        [key_grad.reshape(-1, head_cols), value_grad.reshape(-1, head_cols)], axis=1
    )
    weight_grads = lax.psum_scatter(
        lax.dot_general(
            flat_rows, both_grads, (((0,), (0,)), ((), ())), preferred_element_type=jnp.float32
        ),
        "dp",
        scatter_dimension=0,
        tiled=True,
    )
    slot_partial = jnp.dot(both_grads, both_weights.T, preferred_element_type=jnp.float32).reshape(
        slot_count, NTOK, E
    )
    slot_grad = lax.psum_scatter(
        slot_partial.astype(jnp.bfloat16), "head", scatter_dimension=2, tiled=True
    )
    quarter = slot_grad.shape[2]
    outgoing = (
        jnp.zeros((dp_count, capacity, NTOK, quarter), jnp.bfloat16)
        .at[owner_dev, slot_rank]
        .set(slot_grad)
    )
    returned = lax.all_to_all(outgoing, "dp", split_axis=0, concat_axis=0, tiled=True)
    block_match = (
        local_index.reshape(-1)[None, :] == jnp.arange(own_blocks, dtype=jnp.int32)[:, None]
    )
    target = (block_match & valid_mask.reshape(-1)[None, :]).astype(jnp.bfloat16)
    encodings_grad = jnp.dot(
        target, returned.reshape(dp_count * capacity, -1), preferred_element_type=jnp.float32
    )
    encodings_grad = encodings_grad.reshape(own_blocks, NTOK, quarter).astype(jnp.bfloat16)
    return (
        query_input_grad,
        encodings_grad,
        weight_grads[:, :head_cols],
        weight_grads[:, head_cols:],
    )

MESH = pl.DeviceIdType.MESH
VMEM_LIMIT = 60 * 1024 * 1024


def remote(src, dst, send_sem, recv_sem, device):
    return pltpu.make_async_remote_copy(
        src_ref=src,
        dst_ref=dst,
        send_sem=send_sem,
        recv_sem=recv_sem,
        device_id=device,
        device_id_type=MESH,
    )


def greet(devices):
    barrier = pltpu.get_barrier_semaphore()
    for device in devices:
        pl.semaphore_signal(barrier, inc=1, device_id=device, device_id_type=MESH)
    pl.semaphore_wait(barrier, len(devices))


def places_kernel(n, mine_ref, all_ref, landed, send_sem, recv_sem):
    me = lax.axis_index("dp")
    greet([{"dp": lax.rem(me + k, n)} for k in range(1, n)])
    copies = []
    for k in range(1, n):
        copy = remote(
            mine_ref,
            landed.at[me],
            send_sem.at[k - 1],
            recv_sem.at[k - 1],
            {"dp": lax.rem(me + k, n)},
        )
        copy.start()
        copies.append(copy)
    for k in range(1, n):
        sender = lax.rem(me - k + n, n)
        remote(
            mine_ref, landed.at[sender], send_sem.at[k - 1], recv_sem.at[k - 1], {"dp": sender}
        ).wait_recv()
        all_ref[sender] = landed[sender]
    all_ref[me] = mine_ref[...]
    for copy in copies:
        copy.wait_send()


def gather_steps(n, packed, got, local_sem, a_sem, y_sem, s_sem, f_sem, ready, project):
    me = lax.axis_index("dp")
    col = lax.axis_index("head")
    far = lax.rem(col + 2, 4)
    near = col + 1 - 2 * lax.rem(col, 2)
    far_near = lax.rem(near + 2, 4)
    ahead = 3

    def first(k):
        there = lax.rem(me + k, n)
        return remote(
            packed.at[there], got.at[me, col], a_sem.at[0, k], a_sem.at[1, k], {"dp": there}
        )

    def arrived(k):
        sender = lax.rem(me - k + n, n)
        return remote(
            packed.at[sender], got.at[sender, col], a_sem.at[0, k], a_sem.at[1, k], {"dp": sender}
        )

    def across(k, feature, sems, target):
        block = got.at[lax.rem(me - k + n, n), feature]
        return remote(block, block, sems.at[0, k], sems.at[1, k], {"head": target})

    own = pltpu.make_async_copy(packed.at[me], got.at[me, col], local_sem)
    own.start()
    for k in range(1, min(n, 1 + ahead)):
        first(k).start()
    own.wait()

    def spread(k):
        across(k, col, y_sem, far).start()
        across(k, col, s_sem, near).start()

    def pass_on(k):
        across(k, far, y_sem, far).wait_recv()
        across(k, far, f_sem, near).start()

    def take(k):
        across(k, near, s_sem, near).wait_recv()
        across(k, far_near, f_sem, near).wait_recv()
        project(lax.rem(me - k + n, n))

    spread(0)
    for k in range(1, n):
        arrived(k).wait_recv()
        spread(k)
        if k + ahead < n:
            first(k + ahead).start()
    pass_on(0)
    ready()

    def step(k, carry):
        pass_on(k)
        take(k - 1)
        return carry

    lax.fori_loop(1, n, step, 0)
    take(n - 1)

    def finish():
        for k in range(n):
            if k:
                first(k).wait_send()
            across(k, col, y_sem, far).wait_send()
            across(k, col, s_sem, near).wait_send()
            across(k, far, f_sem, near).wait_send()

    return finish


def dot(a, b, over_a, over_b):
    return lax.dot_general(
        a, b, (((over_a,), (over_b,)), ((), ())), preferred_element_type=jnp.float32
    )


def exchange_kernel(
    n,
    cap,
    dev_ref,
    rank_ref,
    slot_ref,
    packed_ref,
    q_hbm,
    g_hbm,
    qw_hbm,
    wk_hbm,
    wv_hbm,
    qi_ref,
    ret_ref,
    kw_ref,
    vw_ref,
    got,
    kv,
    blocks,
    grads,
    dq,
    q,
    g,
    qw,
    wkv,
    load_sem,
    local_sem,
    ga_sem,
    gy_sem,
    gs_sem,
    gf_sem,
    s_terms,
    s_in,
    s_far,
    s_far_in,
    s_sum,
    s_back,
    s_back_in,
    q_own,
    q_out,
    q_in,
    q_far,
    q_far_in,
    w_own,
    w_out,
    w_in,
    w_far,
    w_far_in,
    ss_sem,
    sy_sem,
    a_sem,
    qs_sem,
    qy_sem,
    wx_sem,
    wz_sem,
):
    me = lax.axis_index("dp")
    col = lax.axis_index("head")
    high, low = col // 2, lax.rem(col, 2)
    far = {"head": lax.rem(col + 2, 4)}
    near = {"head": col + 1 - 2 * low}
    side, line = lax.rem(me, 2), me // 2
    lines = n // 2
    pair = {"dp": me + 1 - 2 * side}
    cols = wk_hbm.shape[1]
    loads = [
        pltpu.make_async_copy(src, dst, load_sem.at[i])
        for i, (src, dst) in enumerate(
            [
                (wk_hbm, wkv.at[:, pl.ds(0, cols)]),
                (wv_hbm, wkv.at[:, pl.ds(cols, cols)]),
                (q_hbm, q),
                (g_hbm, g),
                (qw_hbm, qw),
            ]
        )
    ]
    for load in loads:
        load.start()
    greet([{"dp": lax.rem(me + k, n)} for k in range(1, n)] + [far, near])
    s_groups, quarter, s_cols = s_far.shape
    q_groups, q_rows, q_cols = q_far.shape
    w_groups, w_rows, w_cols = w_own.shape[0], w_own.shape[2], w_own.shape[3]

    def f32(x):
        return x.astype(jnp.float32)

    def project(sender):
        rows = jnp.concatenate(
            [got[sender, :, r].reshape(wkv.shape[0], NTOK) for r in range(cap)], axis=1
        )
        kv[sender] = dot(rows, wkv[...], 0, 0).astype(jnp.bfloat16).reshape(cap, NTOK, 2 * cols)

    def weights_ready():
        for load in loads[:2]:
            load.wait()

    gather_sent = gather_steps(
        n, packed_ref, got, local_sem, ga_sem, gy_sem, gs_sem, gf_sem, weights_ready, project
    )
    for load in loads[2:]:
        load.wait()

    def span(c):
        places = [(dev_ref[NEIGH * c + j], rank_ref[NEIGH * c + j]) for j in range(NEIGH)]
        keys = NEIGH * NTOK
        for j, (dev, rank) in enumerate(places):
            at = pl.ds(pl.multiple_of(c * keys + j * NTOK, NTOK), NTOK)
            blocks[:, :, :, at] = got[dev, :, rank].reshape(lines, 2, -1, NTOK)
        both = jnp.concatenate([kv[dev, rank] for dev, rank in places], axis=0)
        token_at = pl.ds(pl.multiple_of(c * CH, CH), CH)
        key_at = pl.ds(pl.multiple_of(c * keys, keys), keys)
        heads = [slice(h * DH, (h + 1) * DH) for h in range(cols // DH)]
        blank = jnp.zeros((CH, DH), jnp.bfloat16)
        corners = [
            jnp.concatenate(
                [
                    jnp.concatenate([q[token_at, at], blank], axis=1),
                    jnp.concatenate([blank, g[token_at, at]], axis=1),
                ],
                axis=0,
            )
            for at in heads
        ]
        scale = 1.0 / math.sqrt(DH)
        products = [
            dot(
                corner,
                jnp.concatenate([both[:, at], both[:, cols + at.start : cols + at.stop]], axis=1),
                1,
                1,
            )
            for corner, at in zip(corners, heads)
        ]
        scores = jnp.concatenate([product[:CH] for product in products], axis=0) * scale
        dprobs = jnp.concatenate([product[CH:] for product in products], axis=0)
        shifted = jnp.exp(scores - jnp.max(scores, axis=-1, keepdims=True))
        probs = shifted * (1.0 / jnp.sum(shifted, axis=-1, keepdims=True))
        delta = jnp.sum(probs * dprobs, axis=-1, keepdims=True)
        dscores = (probs * (dprobs - delta) * scale).astype(jnp.bfloat16)
        half = probs.astype(jnp.bfloat16)
        for h, at in enumerate(heads):
            rows = slice(h * CH, (h + 1) * CH)
            pair_rows = jnp.concatenate([dscores[rows], half[rows]], axis=0)
            grad = dot(pair_rows, corners[h], 0, 0).astype(jnp.bfloat16)
            grads[key_at, at] = grad[:, :DH]
            grads[key_at, cols + at.start : cols + at.stop] = grad[:, DH:]
            dq[token_at, at] = dot(dscores[rows], both[:, at], 1, 0).astype(jnp.bfloat16)

    def near_copy(out, landed, sems, i):
        return remote(out.at[i], landed.at[i], sems.at[0, i], sems.at[1, i], near)

    def far_copy(out, landed, sems, i):
        return remote(out.at[i], landed.at[i], sems.at[0, i], sems.at[1, i], far)

    def slot_terms(i):
        at = pl.ds(pl.multiple_of(i * s_cols, s_cols), s_cols)
        terms = dot(wkv[...], grads[at, :], 1, 1).astype(jnp.bfloat16)
        for owner in range(4):
            s_terms[i, owner % 2, owner // 2] = terms[owner * quarter : (owner + 1) * quarter]
        slot_copy(i).start()

    def slot_copy(i):
        return remote(
            s_terms.at[i, 1 - low], s_in.at[i], ss_sem.at[0, i], ss_sem.at[1, i], near
        )

    def slot_pairs(i):
        slot_copy(i).wait_recv()
        s_far[i] = (f32(s_terms[i, low, 1 - high]) + f32(s_in[i, 1 - high])).astype(jnp.bfloat16)
        far_copy(s_far, s_far_in, sy_sem, i).start()

    def slot_sums(i):
        far_copy(s_far, s_far_in, sy_sem, i).wait_recv()
        total = (f32(s_terms[i, low, high]) + f32(s_in[i, high]) + f32(s_far_in[i])).astype(jnp.bfloat16)
        per = s_cols // NTOK
        for j in range(per):
            s_sum[i * per + j] = total[:, j * NTOK : (j + 1) * NTOK]

    def query_terms(i):
        for part in range(2):
            for target, owner in ((q_out, 1 - low), (q_own, low)):
                start = (2 * part + owner) * (q_groups * q_cols) + i * q_cols
                rows = pl.ds(pl.multiple_of(start, q_cols), q_cols)
                target[i, part] = dot(dq[...], qw[rows, :], 1, 1).astype(jnp.bfloat16)
        near_copy(q_out, q_in, qs_sem, i).start()

    def query_pairs(i):
        near_copy(q_out, q_in, qs_sem, i).wait_recv()
        q_far[i] = (f32(q_own[i, 1 - high]) + f32(q_in[i, 1 - high])).astype(jnp.bfloat16)
        far_copy(q_far, q_far_in, qy_sem, i).start()

    def query_sums(i):
        far_copy(q_far, q_far_in, qy_sem, i).wait_recv()
        at = pl.ds(pl.multiple_of(i * q_cols, q_cols), q_cols)
        qi_ref[:, at] = (f32(q_own[i, high]) + f32(q_in[i, high]) + f32(q_far_in[i])).astype(
            jnp.bfloat16
        )

    def weight_copy(i):
        return remote(w_out.at[i], w_in.at[i], wx_sem.at[0, i], wx_sem.at[1, i], pair)

    def weight_send(i):
        at = pl.ds(pl.multiple_of(i * w_cols, w_cols), w_cols)
        rows = blocks[...].reshape(2 * lines * w_rows, blocks.shape[3])
        terms = dot(rows, grads[:, at], 1, 0).reshape(lines, 2, w_rows, w_cols)
        for which in range(2):

            @pl.when(side == which)
            def _():
                w_out[i] = terms[:, 1 - which].astype(jnp.bfloat16)
                w_own[i] = terms[:, which]

        weight_copy(i).start()

    def line_copy(i, k, sign):
        there = 2 * lax.rem(line + sign * k + lines, lines) + side
        return remote(
            w_far.at[i, k - 1],
            w_far_in.at[i, k - 1],
            wz_sem.at[0, i, k - 1],
            wz_sem.at[1, i, k - 1],
            {"dp": there},
        )

    def weight_pairs(i):
        weight_copy(i).wait_recv()
        for k in range(1, lines):
            there = lax.rem(line + k, lines)
            w_far[i, k - 1] = (w_own[i, there] + f32(w_in[i, there])).astype(jnp.bfloat16)
            line_copy(i, k, 1).start()

    def weight_sums(i):
        total = w_own[i, line] + f32(w_in[i, line])
        for k in range(1, lines):
            line_copy(i, k, -1).wait_recv()
            total = total + f32(w_far_in[i, k - 1])
        return total

    def back_copy(k):
        return remote(
            s_back.at[k - 1],
            s_back_in.at[k - 1],
            a_sem.at[0, k - 1],
            a_sem.at[1, k - 1],
            {"dp": lax.rem(me + k, n)},
        )

    def loop(start, count, body):
        def step(i, carry):
            body(i)
            return carry

        lax.fori_loop(start, count, step, 0)

    per_group = s_cols // (NEIGH * NTOK)

    def group(i):
        loop(i * per_group, (i + 1) * per_group, span)
        slot_terms(i)

    def group_step(i):
        group(i)
        slot_pairs(i - 1)

    group(0)
    loop(1, s_groups, group_step)
    weight_send(0)
    slot_pairs(s_groups - 1)
    early = q_groups // 2

    def early_step(i):
        query_terms(i)
        weight_send(i + 1)
        query_pairs(i)

    loop(0, early, early_step)
    loop(early + 1, w_groups, weight_send)
    loop(0, s_groups, slot_sums)
    for k in range(1, n):
        there = lax.rem(me + k, n)
        for r in range(cap):
            s_back[k - 1, r] = s_sum[slot_ref[there * cap + r]]
        back_copy(k).start()
    for r in range(cap):
        ret_ref[me, r] = s_sum[slot_ref[me * cap + r]]

    def late_step(i):
        query_terms(early + i)
        weight_pairs(i)
        query_pairs(early + i)

    loop(0, q_groups - early, late_step)

    def last_step(i):
        weight_pairs(i)

    loop(q_groups - early, w_groups, last_step)
    loop(0, q_groups, query_sums)
    for i in range(w_groups):
        total = weight_sums(i)
        at = i * w_cols
        out, at = (kw_ref, at) if at < cols else (vw_ref, at - cols)
        out[:, at : at + w_cols] = total
    for k in range(1, n):
        back_copy(k).wait_recv()
        ret_ref[lax.rem(me - k + n, n)] = s_back_in[k - 1]

    def sent(i):
        slot_copy(i).wait_send()
        far_copy(s_far, s_far_in, sy_sem, i).wait_send()

    loop(0, s_groups, sent)

    def query_sent(i):
        near_copy(q_out, q_in, qs_sem, i).wait_send()
        far_copy(q_far, q_far_in, qy_sem, i).wait_send()

    loop(0, q_groups, query_sent)

    def weight_sent(i):
        weight_copy(i).wait_send()
        for k in range(1, lines):
            line_copy(i, k, 1).wait_send()

    loop(0, w_groups, weight_sent)
    for k in range(1, n):
        back_copy(k).wait_send()
    gather_sent()


def scatter_kernel(
    index_ref, ret_ref, qi_in, kw_in, vw_in, out_ref, qi_out, kw_out, vw_out, total
):
    qi_out[...] = qi_in[...]
    kw_out[...] = kw_in[...]
    vw_out[...] = vw_in[...]
    total[...] = jnp.zeros_like(total)
    senders, cap = ret_ref.shape[:2]

    def add(i, carry):
        place = index_ref[i]

        @pl.when(place >= 0)
        def _():
            at = jnp.maximum(place, 0)
            total[at] += ret_ref[i // cap, i % cap].astype(jnp.float32)

        return carry

    lax.fori_loop(0, senders * cap, add, 0)

    def turn(i, carry):
        out_ref[i] = total[i].astype(jnp.bfloat16)
        return carry

    lax.fori_loop(0, total.shape[0], turn, 0)


def call(kernel, out_shape, scratch, collective=None, **kwargs):
    params = dict(vmem_limit_bytes=VMEM_LIMIT)
    if collective is not None:
        params.update(collective_id=collective, has_side_effects=True)
    return pl.pallas_call(
        kernel,
        out_shape=out_shape,
        scratch_shapes=scratch,
        compiler_params=pltpu.CompilerParams(**params),
        **kwargs,
    )


def shards(
    queries,
    encodings,
    neighbour_ids,
    block_place,
    query_weight,
    key_weight,
    value_weight,
    attn_grad,
):
    n = lax.axis_size("dp")
    bf16, f32, i32 = jnp.bfloat16, jnp.float32, jnp.int32
    own_blocks, _, quarter = encodings.shape
    spans = neighbour_ids.shape[0]
    slots = spans * NEIGH
    cap = -(-slots // n)
    me = lax.axis_index("dp")
    cols = key_weight.shape[1]
    depth = key_weight.shape[0]
    vmem = pl.BlockSpec(memory_space=pltpu.VMEM)
    anywhere = pl.BlockSpec(memory_space=pl.ANY)
    dma = pltpu.SemaphoreType.DMA
    sds = jax.ShapeDtypeStruct

    position = block_place[neighbour_ids.reshape(-1)]
    padded = jnp.zeros((8, 128), i32).at[0, :slots].set(position)
    places = call(
        functools.partial(places_kernel, n),
        sds((n, 8, 128), i32),
        [pltpu.VMEM((n, 8, 128), i32), dma((n - 1,)), dma((n - 1,))],
        collective=0,
        in_specs=[vmem],
        out_specs=vmem,
    )(padded)[:, 0, :slots]

    earlier = jnp.arange(slots, dtype=i32)[None, :] < jnp.arange(slots, dtype=i32)[:, None]
    ranks = jnp.arange(cap, dtype=i32)
    mine = (places // own_blocks) == me
    asked_rank = jnp.sum((mine[:, None, :] & earlier[None]).astype(i32), axis=2)
    pick = mine[:, None, :] & (asked_rank[:, None, :] == ranks[None, :, None])
    asked = jnp.sum(jnp.where(pick, (places % own_blocks)[:, None, :] + 1, 0), axis=2) - 1
    owner = position // own_blocks
    rank = jnp.sum(((owner[:, None] == owner[None, :]) & earlier).astype(i32), axis=1)
    chosen = (owner[None, None, :] == jnp.arange(n, dtype=i32)[:, None, None]) & (
        rank[None, None, :] == ranks[None, :, None]
    )
    slot_at = jnp.sum(jnp.where(chosen, jnp.arange(slots, dtype=i32), 0), axis=2).reshape(-1)

    packed = jnp.swapaxes(encodings, 1, 2)[jnp.maximum(asked, 0)]
    tokens = slots * NTOK
    lines, w_rows, groups = n // 2, depth // n, 4
    s_cols = tokens // groups
    q_rows = queries.shape[0]
    q_width = query_weight.shape[0] // 4
    q_cols = q_width // groups
    w_cols = 2 * cols // groups

    def buffer(*shape, dtype=bf16):
        return pltpu.VMEM(shape, dtype)

    scratch = [
        buffer(n, 4, cap, quarter, NTOK),
        buffer(n, cap, NTOK, 2 * cols),
        buffer(lines, 2, w_rows, tokens),
        buffer(tokens, 2 * cols),
        buffer(q_rows, cols),
        buffer(q_rows, cols),
        buffer(q_rows, cols),
        buffer(*query_weight.shape),
        buffer(depth, 2 * cols),
        dma((5,)),
        dma,
        dma((2, n)),
        dma((2, n)),
        dma((2, n)),
        dma((2, n)),
        buffer(groups, 2, 2, quarter, s_cols),
        buffer(groups, 2, quarter, s_cols),
        buffer(groups, quarter, s_cols),
        buffer(groups, quarter, s_cols),
        buffer(slots, quarter, NTOK),
        buffer(n - 1, cap, quarter, NTOK),
        buffer(n - 1, cap, quarter, NTOK),
        buffer(groups, 2, q_rows, q_cols),
        buffer(groups, 2, q_rows, q_cols),
        buffer(groups, 2, q_rows, q_cols),
        buffer(groups, q_rows, q_cols),
        buffer(groups, q_rows, q_cols),
        buffer(groups, lines, w_rows, w_cols, dtype=f32),
        buffer(groups, lines, w_rows, w_cols),
        buffer(groups, lines, w_rows, w_cols),
        buffer(groups, lines - 1, w_rows, w_cols),
        buffer(groups, lines - 1, w_rows, w_cols),
        dma((2, groups)),
        dma((2, groups)),
        dma((2, n - 1)),
        dma((2, groups)),
        dma((2, groups)),
        dma((2, groups)),
        dma((2, groups, lines - 1)),
    ]
    query_input_grad, returned, key_grad, value_grad = call(
        functools.partial(exchange_kernel, n, cap),
        [
            sds((q_rows, q_width), bf16),
            sds((n, cap, quarter, NTOK), bf16),
            sds((w_rows, cols), f32),
            sds((w_rows, cols), f32),
        ],
        scratch,
        collective=1,
        in_specs=[pl.BlockSpec(memory_space=pltpu.SMEM)] * 3 + [vmem] + [anywhere] * 5,
        out_specs=[vmem] * 4,
    )(
        owner,
        rank,
        slot_at,
        packed,
        queries,
        attn_grad,
        query_weight,
        key_weight,
        value_weight,
    )
    encodings_grad, query_input_grad, key_grad, value_grad = call(
        scatter_kernel,
        [
            sds((own_blocks, quarter, NTOK), bf16),
            sds(query_input_grad.shape, bf16),
            sds(key_grad.shape, f32),
            sds(value_grad.shape, f32),
        ],
        [pltpu.VMEM((own_blocks, quarter, NTOK), f32)],
        in_specs=[pl.BlockSpec(memory_space=pltpu.SMEM), vmem, vmem, vmem, vmem],
        out_specs=[vmem] * 4,
    )(asked.reshape(-1), returned, query_input_grad, key_grad, value_grad)
    return query_input_grad, jnp.swapaxes(encodings_grad, 1, 2), key_grad, value_grad


def fits(mesh):
    dp, head = mesh.shape["dp"], mesh.shape["head"]
    return head == 4 and dp % 2 == 0 and dp > 2 and E % (16 * dp) == 0


def solution(mesh):
    in_specs = (
        P("dp", "head"),
        P("dp", None, "head"),
        P("dp", None),
        P(),
        P(None, "head"),
        P(None, "head"),
        P(None, "head"),
        P("dp", "head"),
    )
    out_specs = (P("dp", "head"), P("dp", None, "head"), P("dp", "head"), P("dp", "head"))
    return jax.shard_map(
        shards if fits(mesh) else plain_shards,
        mesh=mesh,
        in_specs=in_specs,
        out_specs=out_specs,
        check_vma=False,
    )
```
